32 devices in a mesh: parts: 2 (over x), kv: 2 (over core), req: 8 (over z, y).
Axes of the slice: x: 2, y: 2, z: 4, core: 2. Of those that a mesh axis runs over, the one named last changes fastest.
Arguments:
- hidden: bfloat16 [16, 16384], P(('parts', 'req')), parts along dimension 0, may hold values from -6 to 6
- norm_gain: float32 [16384], replicated, may hold values from 0.1 to 1.9
- w_query: bfloat16 [16384, 2, 2048], P('req', 'kv'), may hold values from -0.046875 to 0.046875
- w_keyval: bfloat16 [16384, 2, 256], P('req', 'kv'), may hold values from -0.046875 to 0.046875
- w_out: bfloat16 [2, 2048, 16384], P('kv', None, 'req'), may hold values from -0.125 to 0.125
- cache: bfloat16 [2, 384, 512, 256], P('kv', ('parts', 'req')), parts along dimension 1, may hold values from -140 to 140
- slot_request: int32 [384], P(('parts', 'req')), parts along dimension 0, may hold values from -1 to 7, as said below
- slot_block: int32 [384], P(('parts', 'req')), parts along dimension 0, may hold values from -1 to 63
- cache_lengths: int32 [16], P('parts'), parts along dimension 0, may hold values from 1 to 32768, as said below
Outputs:
- attention_out: bfloat16 [16, 16384], P(('parts', 'req')), parts along dimension 0
The draws below stay inside these ranges and needn't reach their ends.
There are 2 independent parts, one for each index of `parts`. The reference program is written for one: setup_inputs(seed, part) draws one part's arguments, and reference() takes and returns one part's arrays. A program takes and returns all parts, laid end to end along the dimension named above; an argument that names none is the same for every part. Nothing has to cross between parts.
Inputs may be any that keep to these rules, and one draw needn't show every extreme that they name: Slot p of a device's 24 slots holds block slot_block[p] of request slot_request[p], or is empty (-1 in both). Every block of request r, that is ceil(cache_lengths[r] / 512) blocks, stands in exactly one slot of the pool; on each device the occupied slots come first. `cache_lengths`: one request has exactly 32768 cached tokens; every other one has at most 8192.
All inputs are finite; a program needn't handle non-finite values.
Results may differ from the reference program's by a relative error of at most 0.007.
The reference program's roundings to bfloat16 on the way (of `normed`, `queries`, `key_value` and `attended`) count: a program that leaves them out, or rounds other values in their place, can miss the bound.
Values may be sent and summed in bfloat16 or wider, within the bound.
No kernel may reach another device: no remote copies, remote signals or barrier semaphores. Data moves between devices by JAX's collectives and lax.ppermute only.
A program may use at most 64 MiB of HBM per device.

```python
import jax
import jax.numpy as jnp
from jax import lax

D = 16384
QPG = 16
HD = 128
SLOTS = 24
BLK = 512
REQS = 8
KV_HEADS = 2
MAX_BLOCKS = 64
OTHER_MOST = 16


def layout(key):
    subkeys = jax.random.split(key, 5)
    request_ids = jnp.arange(REQS, dtype=jnp.int32)
    blocks = jax.random.randint(subkeys[0], (REQS,), 1, OTHER_MOST + 1)
    longest = jax.random.randint(subkeys[1], (), 0, REQS)
    blocks = jnp.where(request_ids == longest, MAX_BLOCKS, blocks)
    tail_tokens = jax.random.randint(subkeys[2], (REQS,), 1, BLK + 1)
    tail_tokens = jnp.where(request_ids == longest, BLK, tail_tokens)
    lengths = (blocks - 1) * BLK + tail_tokens
    request_order = jax.random.permutation(subkeys[3], REQS)
    ordered_blocks = blocks[request_order]
    block_ends = jnp.cumsum(ordered_blocks)
    block_starts = block_ends - ordered_blocks
    pool_slot = jnp.arange(REQS * SLOTS, dtype=jnp.int32)
    pool_rank = jnp.minimum(jnp.sum((pool_slot[:, None] >= block_ends[None, :]).astype(jnp.int32), axis=1), REQS - 1)
    occupied = pool_slot < block_ends[REQS - 1]
    slot_owner = jnp.where(occupied, request_order[pool_rank], -1)
    slot_index = jnp.where(occupied, pool_slot - block_starts[pool_rank], -1)
    device_order = jax.random.permutation(subkeys[4], REQS)
    slot_owner = slot_owner.reshape(REQS, SLOTS)[device_order].reshape(-1)
    slot_index = slot_index.reshape(REQS, SLOTS)[device_order].reshape(-1)
    return (slot_owner, slot_index, lengths)


def draw_slot_request(key, part):
    shared = layout(key)
    return shared[0].astype(jnp.int32)


def draw_slot_block(key, part):
    shared = layout(key)
    return shared[1].astype(jnp.int32)


def draw_cache_lengths(key, part):
    shared = layout(key)
    return shared[2].astype(jnp.int32)


def draw_cache(key, part):
    key = jax.random.fold_in(key, 7)
    subkeys = jax.random.split(key, 1)
    cache_shape = (KV_HEADS, REQS * SLOTS, BLK, 2 * HD)
    values = jnp.clip(jax.random.normal(subkeys[0], cache_shape, jnp.float32), -6.0, 6.0)
    return values.astype(jnp.bfloat16)


def levels(stream_key, shape, shards, low, high):
    gain, own = 1.0, jax.random.fold_in(stream_key, 6)
    for axis_at, shards_of in shards:
        heights = jnp.exp(jax.random.uniform(jax.random.fold_in(own, axis_at), (shards_of,), jnp.float32, low / len(shards), high / len(shards)))
        gain = gain * jnp.repeat(heights, shape[axis_at] // shards_of).reshape([-1 if axis == axis_at else 1 for axis in range(len(shape))])
    return gain


def noise(stream_key, shape, scale, limit, shards=(), held_as=jnp.bfloat16):
    level = levels(stream_key, shape, shards, -0.22, 0.18) if shards else 1.0
    drawn = jax.random.normal(stream_key, shape, jnp.float32) * scale * level
    return jnp.minimum(jnp.maximum(drawn, -limit), limit).astype(held_as)


def setup_inputs(seed: int = 0, part: int = 0) -> dict:
    arg_keys = jax.random.split(jax.random.key(seed), 10)
    own_keys = jax.random.split(jax.random.fold_in(arg_keys[9], part), 10)
    return {
        "hidden": noise(own_keys[0], (REQS, D), 1.0, 6.0, ((0, 8),)),
        "norm_gain": jnp.clip(1.0 + 0.18 * jax.random.normal(arg_keys[1], (D,), jnp.float32), 0.1, 1.9),
        "w_query": noise(arg_keys[2], (D, KV_HEADS, QPG * HD), D ** -0.5, 0.046875, ((0, 8), (1, 2))),
        "w_keyval": noise(arg_keys[3], (D, KV_HEADS, 2 * HD), D ** -0.5, 0.046875, ((0, 8), (1, 2))),
        "w_out": noise(arg_keys[4], (KV_HEADS, QPG * HD, D), (QPG * HD) ** -0.5, 0.125, ((0, 2), (2, 8))),
        "cache": draw_cache(jax.random.fold_in(jax.random.fold_in(arg_keys[9], part), 71), part),
        "slot_request": draw_slot_request(jax.random.fold_in(jax.random.fold_in(arg_keys[9], part), 71), part),
        "slot_block": draw_slot_block(jax.random.fold_in(jax.random.fold_in(arg_keys[9], part), 71), part),
        "cache_lengths": draw_cache_lengths(jax.random.fold_in(jax.random.fold_in(arg_keys[9], part), 71), part),
    }


def reference(hidden, norm_gain, w_query, w_keyval, w_out, cache, slot_request, slot_block, cache_lengths):
    highest = lax.Precision.HIGHEST
    activations = hidden.astype(jnp.float32)
    normed = (activations * lax.rsqrt(lax.optimization_barrier(jnp.mean(activations * activations, axis=1, keepdims=True)) + 1e-05) * norm_gain).astype(jnp.bfloat16)
    queries = jnp.dot(normed, w_query.reshape(D, -1), preferred_element_type=jnp.float32).astype(jnp.bfloat16).reshape(REQS, KV_HEADS, QPG, HD)
    key_value = jnp.dot(normed, w_keyval.reshape(D, -1), preferred_element_type=jnp.float32).astype(jnp.bfloat16).reshape(REQS, KV_HEADS, 2 * HD)
    slot_owner = jnp.maximum(slot_request, 0)
    positions = slot_block[:, None] * BLK + jnp.arange(BLK, dtype=jnp.int32)[None, :]
    live_tokens = (slot_request >= 0)[:, None] & (positions < cache_lengths[slot_owner][:, None])
    score_scale = HD ** (-0.5)
    projected = jnp.zeros((REQS, D), jnp.float32)
    for head_group in range(KV_HEADS):
        slot_query = queries[slot_owner, head_group].astype(jnp.float32)
        block_keys = cache[head_group, :, :, :HD].astype(jnp.float32)
        block_values = cache[head_group, :, :, HD:].astype(jnp.float32)
        scores = jnp.einsum('phd,ptd->pht', slot_query, block_keys, precision=highest) * score_scale
        masked = jnp.where(live_tokens[:, None, :], scores, -1e+30)
        block_max = lax.optimization_barrier(jnp.max(masked, axis=2))
        weights = jnp.where(live_tokens[:, None, :], jnp.exp(masked - block_max[:, :, None]), 0.0)
        block_sum = lax.optimization_barrier(jnp.sum(weights, axis=2))
        rounded = lax.optimization_barrier(weights.astype(jnp.bfloat16))
        block_out = jnp.einsum('pht,ptd->phd', rounded.astype(jnp.float32), block_values, precision=highest)
        new_key = key_value[:, head_group, :HD].astype(jnp.float32)
        new_value = key_value[:, head_group, HD:].astype(jnp.float32)
        own_score = jnp.einsum('rhd,rd->rh', queries[:, head_group].astype(jnp.float32), new_key, precision=highest) * score_scale

        def per_request(request):
            chosen = slot_request == request
            top_score = jnp.maximum(lax.optimization_barrier(jnp.max(jnp.where(chosen[:, None], block_max, -1e+30), axis=0)), own_score[request])
            factor = jnp.where(chosen[:, None], jnp.exp(block_max - top_score[None, :]), 0.0)
            own_factor = jnp.exp(own_score[request] - top_score)
            denominator = own_factor + lax.optimization_barrier(jnp.sum(factor * block_sum, axis=0))
            summed = own_factor[:, None] * new_value[request][None, :] + lax.optimization_barrier(jnp.sum(factor[:, :, None] * block_out, axis=0))
            return (summed / denominator[:, None]).astype(jnp.bfloat16)
        attended = lax.map(per_request, jnp.arange(REQS, dtype=jnp.int32))
        projected = projected + jnp.dot(attended.reshape(REQS, QPG * HD), w_out[head_group], preferred_element_type=jnp.float32)
    return projected.astype(jnp.bfloat16)
```

```python
import functools

import jax
import jax.numpy as jnp
from jax import lax
from jax.experimental import pallas as pl
from jax.experimental.pallas import tpu as pltpu
from jax.sharding import PartitionSpec as P

LANES = 128
EMPTY = -1e30
F32 = jnp.float32
BF16 = jnp.bfloat16
VMEM = pl.BlockSpec(memory_space=pltpu.VMEM)
SMEM = pl.BlockSpec(memory_space=pltpu.SMEM)
MIB = 1024 * 1024


def norm_kernel(hidden_ref, gain_ref, out_ref, rows):
    count = rows.shape[0]
    for row in range(count):
        rows[row : row + 1, :] = hidden_ref[:, row * LANES : (row + 1) * LANES].astype(F32)
    x = rows[...]
    mean = jnp.sum(jnp.sum(x * x, axis=0, keepdims=True), axis=1, keepdims=True) / (count * LANES)
    out_ref[...] = (x * lax.rsqrt(mean + 1e-05) * gain_ref[...]).astype(BF16)


def project_kernel(x_ref, query_ref, pair_ref, out_ref):
    x = x_ref[...].astype(F32)
    x = jnp.concatenate([x[:, chunk, :] for chunk in range(x.shape[1])], axis=1).astype(BF16)
    width = query_ref.shape[1]
    step = 512
    for at in range(0, width, step):
        out_ref[:, at : at + step] = jnp.dot(
            x, query_ref[:, at : at + step], preferred_element_type=F32
        )
    out_ref[:, width:] = jnp.dot(x, pair_ref[...], preferred_element_type=F32)


def attend_kernel(
    me_ref, owner_ref, block_ref, length_ref, mine_ref, other_ref, cache_ref, out_ref,
    wide, query, new_key, new_value, top, total, summed,
):
    requests = mine_ref.shape[0]
    slots, tokens, lanes = cache_ref.shape
    dim = lanes // 2
    heads = (mine_ref.shape[1] - lanes) // dim
    scale = dim ** (-0.5)
    rows = requests * heads
    for head in range(heads):
        at = slice(head * dim, (head + 1) * dim)
        wide[pl.ds(head, requests, stride=heads), :] = mine_ref[:, at] + other_ref[:, at]
    query[...] = wide[...].astype(BF16)
    for new, start in ((new_key, heads * dim), (new_value, heads * dim + dim)):
        at = slice(start, start + dim)
        new[...] = (mine_ref[:, at] + other_ref[:, at]).astype(BF16).astype(F32)

    me = me_ref[0]
    mine = pl.ds(pl.multiple_of(me * heads, heads), heads)
    own_key = new_key[pl.ds(me, 1), :]
    own_value = new_value[pl.ds(me, 1), :]
    own_score = (
        jnp.sum(query[mine, :].astype(F32) * own_key, axis=1, keepdims=True) * scale
    )
    top[...] = jnp.full(top.shape, EMPTY, F32)
    total[...] = jnp.zeros(total.shape, F32)
    summed[...] = jnp.zeros(summed.shape, F32)
    top[mine, :] = jnp.broadcast_to(own_score, (heads, dim))

    token = lax.broadcasted_iota(jnp.int32, (heads, tokens), 1)
    places = []
    maxima = []
    sums = []
    outs = []
    for slot in range(slots):
        owner = owner_ref[slot]
        used = owner >= 0
        source = jnp.maximum(owner, 0)
        live = jnp.where(used, length_ref[source] - block_ref[slot] * tokens, 0)
        scores = (
            lax.dot_general(
                query[pl.ds(pl.multiple_of(source * heads, heads), heads), :],
                cache_ref[slot, :, :dim],
                (((1,), (1,)), ((), ())),
                preferred_element_type=F32,
            )
            * scale
        )
        masked = jnp.where(token < live, scores, EMPTY)
        block_max = jnp.max(masked, axis=1, keepdims=True)
        weights = jnp.exp(masked - block_max)
        block_sum = jnp.sum(weights, axis=1, keepdims=True)
        block_out = jnp.dot(
            weights.astype(BF16), cache_ref[slot, :, dim:], preferred_element_type=F32
        )
        places.append(pl.ds(pl.multiple_of(jnp.where(used, owner, requests) * heads, heads), heads))
        maxima.append(jnp.broadcast_to(block_max, (heads, dim)))
        sums.append(jnp.broadcast_to(block_sum, (heads, dim)))
        outs.append(block_out)
    for place, block_max in zip(places, maxima):
        top[place, :] = jnp.maximum(top[place, :], block_max)
    for place, block_max, block_sum, block_out in zip(places, maxima, sums, outs):
        factor = jnp.exp(block_max - top[place, :])
        total[place, :] = total[place, :] + factor * block_sum
        summed[place, :] = summed[place, :] + factor * block_out
    own_factor = jnp.exp(own_score - top[mine, :])
    total[mine, :] = total[mine, :] + own_factor
    summed[mine, :] = summed[mine, :] + own_factor * own_value

    out_ref[:dim, :] = summed[:rows, :].T
    out_ref[dim : dim + 1, :] = top[:rows, :].T[:1, :]
    out_ref[dim + 1 : dim + 2, :] = total[:rows, :].T[:1, :]
    out_ref[dim + 2 :, :] = jnp.zeros((out_ref.shape[0] - dim - 2, rows), F32)


def merged(first_ref, second_ref):
    dim = LANES
    first_top = first_ref[dim : dim + 1, :]
    second_top = second_ref[dim : dim + 1, :]
    top = jnp.maximum(first_top, second_top)
    first_factor = jnp.exp(first_top - top)
    second_factor = jnp.exp(second_top - top)
    total = (
        first_ref[dim + 1 : dim + 2, :] * first_factor
        + second_ref[dim + 1 : dim + 2, :] * second_factor
    )
    summed = first_ref[:dim, :] * first_factor + second_ref[:dim, :] * second_factor
    return top, total, summed


def merge_kernel(first_ref, second_ref, out_ref):
    dim = LANES
    top, total, summed = merged(first_ref, second_ref)
    out_ref[:dim, :] = summed
    out_ref[dim : dim + 1, :] = top
    out_ref[dim + 1 : dim + 2, :] = total
    out_ref[dim + 2 :, :] = jnp.zeros((out_ref.shape[0] - dim - 2, out_ref.shape[1]), F32)


def output_kernel(first_ref, second_ref, weight_ref, out_ref, rows):
    _, total, summed = merged(first_ref, second_ref)
    rows[...] = (summed / total).T
    heads = weight_ref.shape[0] // LANES
    requests = rows.shape[0] // heads
    x = jnp.concatenate(
        [rows[pl.ds(head, requests, stride=heads), :] for head in range(heads)], axis=1
    ).astype(BF16)
    width = weight_ref.shape[1]
    chunks = width // LANES
    step = min(512, width)
    for at in range(0, width, step):
        y = jnp.dot(x, weight_ref[:, at : at + step], preferred_element_type=F32)
        for chunk in range(step // LANES):
            part = y[:, chunk * LANES : (chunk + 1) * LANES]
            for copy in range(out_ref.shape[0]):
                out_ref[copy, pl.ds(at // LANES + chunk, requests, stride=chunks), :] = part


def call(kernel, shape, dtype, in_specs, scratch=(), limit=4 * MIB, flops=0, moved=0):
    return pl.pallas_call(
        kernel,
        out_shape=jax.ShapeDtypeStruct(shape, dtype),
        in_specs=in_specs,
        out_specs=VMEM,
        scratch_shapes=list(scratch),
        compiler_params=pltpu.CompilerParams(vmem_limit_bytes=limit),
        cost_estimate=pl.CostEstimate(flops=flops, bytes_accessed=moved, transcendentals=0),
    )


def exchanged(x, distance, size):
    return lax.ppermute(x, "req", [(place, place ^ distance) for place in range(size)])


def on_device(
    sizes, hidden, norm_gain, w_query, w_keyval, w_out, cache, slot_request, slot_block, cache_lengths
):
    requests = sizes["req"]
    features = hidden.shape[1]
    feature_rows = features // requests
    query_weight = w_query.reshape(feature_rows, -1)
    pair_weight = w_keyval.reshape(feature_rows, -1)
    head_width = query_weight.shape[1]
    lanes = pair_weight.shape[1]
    dim = lanes // 2
    heads = head_width // dim
    rows = requests * heads
    slots, tokens = cache.shape[1:3]

    normed = call(
        norm_kernel, (features // LANES, LANES), BF16, [VMEM, VMEM],
        [pltpu.VMEM((features // LANES, LANES), F32)],
    )(hidden, norm_gain.reshape(features // LANES, LANES))
    columns = lax.all_to_all(
        normed.reshape(requests, feature_rows // LANES, LANES), "req", 0, 0, tiled=True
    )
    sums = call(
        project_kernel, (requests, head_width + lanes), F32, [VMEM] * 3, limit=16 * MIB,
        flops=2 * requests * feature_rows * (head_width + lanes),
        moved=2 * feature_rows * (head_width + lanes),
    )(columns, query_weight, pair_weight)
    distance = 1
    while distance < requests:
        other = exchanged(sums, distance, requests)
        distance *= 2
        if distance < requests:
            sums = sums + other

    me = lax.axis_index("req").astype(jnp.int32).reshape(1)
    part = call(
        attend_kernel, (dim + 8, rows), F32, [SMEM] * 4 + [VMEM] * 3,
        [
            pltpu.VMEM((rows, dim), F32),
            pltpu.VMEM((rows, dim), BF16),
            pltpu.VMEM((requests, dim), F32),
            pltpu.VMEM((requests, dim), F32),
            pltpu.VMEM((rows + heads, dim), F32),
            pltpu.VMEM((rows + heads, dim), F32),
            pltpu.VMEM((rows + heads, dim), F32),
        ],
        limit=16 * MIB,
        flops=2 * slots * tokens * heads * lanes,
        moved=2 * slots * tokens * lanes,
    )(me, slot_request, slot_block, cache_lengths, sums, other, cache[0])
    distance = 1
    while distance < requests:
        other = exchanged(part, distance, requests)
        distance *= 2
        if distance < requests:
            part = call(merge_kernel, part.shape, F32, [VMEM] * 2)(part, other)

    columns_out = w_out.shape[2]
    projected = call(
        output_kernel, (sizes["kv"], requests * columns_out // LANES, LANES), F32, [VMEM] * 3,
        [pltpu.VMEM((rows, dim), F32)],
        limit=16 * MIB,
        flops=2 * requests * head_width * columns_out,
        moved=2 * head_width * columns_out,
    )(part, other, w_out[0])
    terms = lax.all_to_all(
        projected.reshape(sizes["kv"] * requests, columns_out // LANES, LANES),
        ("kv", "req"), 0, 0, tiled=True,
    )
    terms = terms.reshape(sizes["kv"], -1)
    return jnp.sum(terms, axis=0, keepdims=True).astype(BF16)


def solution(mesh):
    placed = (
        P(("parts", "req"), None),
        P(),
        P("req", "kv", None),
        P("req", "kv", None),
        P("kv", None, "req"),
        P("kv", ("parts", "req"), None, None),
        P(("parts", "req")),
        P(("parts", "req")),
        P("parts"),
    )
    return jax.shard_map(
        functools.partial(on_device, dict(mesh.shape)),
        mesh=mesh, in_specs=placed, out_specs=P(("parts", "req"), None), check_vma=False,
    )
```

```python
import functools

import jax
import jax.numpy as jnp
from jax import lax
from jax.experimental import pallas as pl
from jax.experimental.pallas import tpu as pltpu
from jax.sharding import PartitionSpec as P

LANES = 128
EMPTY = -1e30
F32 = jnp.float32
BF16 = jnp.bfloat16
VMEM = pl.BlockSpec(memory_space=pltpu.VMEM)
SMEM = pl.BlockSpec(memory_space=pltpu.SMEM)
MIB = 1024 * 1024


def spread_kernel(hidden_ref, out_ref):
    for row in range(out_ref.shape[0]):
        out_ref[row : row + 1, :] = hidden_ref[:, row * LANES : (row + 1) * LANES].astype(F32)


def scale_kernel(x_ref, out_ref):
    x = x_ref[...]
    mean = jnp.sum(jnp.sum(x * x, axis=0, keepdims=True), axis=1, keepdims=True) / x.size
    out_ref[...] = x * lax.rsqrt(mean + 1e-05)


def project_kernel(x_ref, gain_ref, query_ref, pair_ref, out_ref):
    chunks = x_ref.shape[1]
    me = lax.axis_index("req").astype(jnp.int32)
    gain = gain_ref[pl.ds(pl.multiple_of(me * chunks, chunks), chunks), :]
    x = x_ref[...] * gain[None]
    x = jnp.concatenate([x[:, chunk, :] for chunk in range(chunks)], axis=1).astype(BF16)
    width = query_ref.shape[1]
    step = 512
    for at in range(0, width, step):
        out_ref[:, at : at + step] = jnp.dot(
            x, query_ref[:, at : at + step], preferred_element_type=F32
        )
    out_ref[:, width:] = jnp.dot(x, pair_ref[...], preferred_element_type=F32)


def attend_kernel(
    owner_ref, block_ref, length_ref, mine_ref, other_ref, cache_ref, out_ref,
    wide, query, new_key, new_value, top, total, summed,
):
    requests = mine_ref.shape[0]
    slots, tokens, lanes = cache_ref.shape
    dim = lanes // 2
    heads = (mine_ref.shape[1] - lanes) // dim
    scale = dim ** (-0.5)
    rows = requests * heads
    for head in range(heads):
        at = slice(head * dim, (head + 1) * dim)
        wide[pl.ds(head, requests, stride=heads), :] = mine_ref[:, at] + other_ref[:, at]
    query[...] = wide[...].astype(BF16)
    for new, start in ((new_key, heads * dim), (new_value, heads * dim + dim)):
        at = slice(start, start + dim)
        new[...] = (mine_ref[:, at] + other_ref[:, at]).astype(BF16).astype(F32)

    me = lax.axis_index("req").astype(jnp.int32)
    mine = pl.ds(pl.multiple_of(me * heads, heads), heads)
    own_key = new_key[pl.ds(me, 1), :]
    own_value = new_value[pl.ds(me, 1), :]
    own_score = (
        jnp.sum(query[mine, :].astype(F32) * own_key, axis=1, keepdims=True) * scale
    )
    top[...] = jnp.full(top.shape, EMPTY, F32)
    total[...] = jnp.zeros(total.shape, F32)
    summed[...] = jnp.zeros(summed.shape, F32)
    top[mine, :] = jnp.broadcast_to(own_score, (heads, dim))

    token = lax.broadcasted_iota(jnp.int32, (heads, tokens), 1)
    owners = [owner_ref[slot] for slot in range(slots)]
    sources = [jnp.maximum(owner, 0) for owner in owners]
    lives = [
        jnp.where(owners[slot] >= 0, length_ref[sources[slot]] - block_ref[slot] * tokens, 0)
        for slot in range(slots)
    ]
    places = [
        pl.ds(pl.multiple_of(jnp.where(owner >= 0, owner, requests) * heads, heads), heads)
        for owner in owners
    ]
    scores = [
        lax.dot_general(
            query[pl.ds(pl.multiple_of(sources[slot] * heads, heads), heads), :],
            cache_ref[slot, :, :dim],
            (((1,), (1,)), ((), ())),
            preferred_element_type=F32,
        )
        for slot in range(slots)
    ]
    masked = [jnp.where(token < lives[slot], scores[slot] * scale, EMPTY) for slot in range(slots)]
    maxima = [jnp.max(masked[slot], axis=1, keepdims=True) for slot in range(slots)]
    for slot in range(slots):
        top[places[slot], :] = jnp.maximum(top[places[slot], :], maxima[slot])
    weights = [jnp.exp(masked[slot] - maxima[slot]) for slot in range(slots)]
    outs = [
        jnp.dot(weights[slot].astype(BF16), cache_ref[slot, :, dim:], preferred_element_type=F32)
        for slot in range(slots)
    ]
    sums = [jnp.sum(weights[slot], axis=1, keepdims=True) for slot in range(slots)]
    factors = [jnp.exp(maxima[slot] - top[places[slot], :]) for slot in range(slots)]
    for slot in range(slots):
        place = places[slot]
        total[place, :] = total[place, :] + factors[slot] * sums[slot]
        summed[place, :] = summed[place, :] + factors[slot] * outs[slot]
    own_factor = jnp.exp(own_score - top[mine, :])
    total[mine, :] = total[mine, :] + own_factor
    summed[mine, :] = summed[mine, :] + own_factor * own_value

    out_ref[:dim, :] = summed[:rows, :].T
    out_ref[dim : dim + 1, :] = top[:rows, :].T[:1, :]
    out_ref[dim + 1 : dim + 2, :] = total[:rows, :].T[:1, :]
    out_ref[dim + 2 :, :] = jnp.zeros((out_ref.shape[0] - dim - 2, rows), F32)


def merged(first_ref, second_ref):
    dim = LANES
    first_top = first_ref[dim : dim + 1, :]
    second_top = second_ref[dim : dim + 1, :]
    top = jnp.maximum(first_top, second_top)
    first_factor = jnp.exp(first_top - top)
    second_factor = jnp.exp(second_top - top)
    total = (
        first_ref[dim + 1 : dim + 2, :] * first_factor
        + second_ref[dim + 1 : dim + 2, :] * second_factor
    )
    summed = first_ref[:dim, :] * first_factor + second_ref[:dim, :] * second_factor
    return top, total, summed


def merge_kernel(first_ref, second_ref, out_ref):
    dim = LANES
    top, total, summed = merged(first_ref, second_ref)
    out_ref[:dim, :] = summed
    out_ref[dim : dim + 1, :] = top
    out_ref[dim + 1 : dim + 2, :] = total
    out_ref[dim + 2 :, :] = jnp.zeros((out_ref.shape[0] - dim - 2, out_ref.shape[1]), F32)


def output_kernel(first_ref, second_ref, weight_ref, out_ref, rows):
    _, total, summed = merged(first_ref, second_ref)
    rows[...] = (summed / total).T
    heads = weight_ref.shape[0] // LANES
    requests = rows.shape[0] // heads
    x = jnp.concatenate(
        [rows[pl.ds(head, requests, stride=heads), :] for head in range(heads)], axis=1
    ).astype(BF16)
    width = weight_ref.shape[1]
    chunks = width // LANES
    step = min(512, width)
    for at in range(0, width, step):
        y = jnp.dot(x, weight_ref[:, at : at + step], preferred_element_type=F32)
        for chunk in range(step // LANES):
            part = y[:, chunk * LANES : (chunk + 1) * LANES]
            for copy in range(out_ref.shape[0]):
                out_ref[copy, pl.ds(at // LANES + chunk, requests, stride=chunks), :] = part


def call(kernel, shape, dtype, in_specs, scratch=(), limit=4 * MIB, flops=0, moved=0):
    return pl.pallas_call(
        kernel,
        out_shape=jax.ShapeDtypeStruct(shape, dtype),
        in_specs=in_specs,
        out_specs=VMEM,
        scratch_shapes=list(scratch),
        compiler_params=pltpu.CompilerParams(vmem_limit_bytes=limit),
        cost_estimate=pl.CostEstimate(flops=flops, bytes_accessed=moved, transcendentals=0),
    )


def exchanged(x, distance, size):
    return lax.ppermute(x, "req", [(place, place ^ distance) for place in range(size)])


def attend(requests, mine, other, cache, slot_request, slot_block, cache_lengths):
    slots, tokens, lanes = cache.shape
    dim = lanes // 2
    heads = (mine.shape[1] - lanes) // dim
    rows = requests * heads
    return call(
        attend_kernel, (dim + 8, rows), F32, [SMEM] * 3 + [VMEM] * 3,
        [
            pltpu.VMEM((rows, dim), F32),
            pltpu.VMEM((rows, dim), BF16),
            pltpu.VMEM((requests, dim), F32),
            pltpu.VMEM((requests, dim), F32),
            pltpu.VMEM((rows + heads, dim), F32),
            pltpu.VMEM((rows + heads, dim), F32),
            pltpu.VMEM((rows + heads, dim), F32),
        ],
        limit=16 * MIB,
        flops=2 * slots * tokens * heads * lanes,
        moved=2 * slots * tokens * lanes,
    )(slot_request, slot_block, cache_lengths, mine, other, cache)


def on_device(
    sizes, hidden, norm_gain, w_query, w_keyval, w_out, cache, slot_request, slot_block, cache_lengths
):
    requests = sizes["req"]
    features = hidden.shape[1]
    feature_rows = features // requests
    query_weight = w_query.reshape(feature_rows, -1)
    pair_weight = w_keyval.reshape(feature_rows, -1)
    head_width = query_weight.shape[1]
    lanes = pair_weight.shape[1]
    dim = lanes // 2
    rows = requests * head_width // dim

    shape = (features // LANES, LANES)
    spread = call(spread_kernel, shape, F32, [VMEM])(hidden)
    scaled = call(scale_kernel, shape, F32, [VMEM], flops=10**11)(spread)
    columns = lax.all_to_all(
        scaled.reshape(requests, feature_rows // LANES, LANES), "req", 0, 0, tiled=True
    )
    sums = call(
        project_kernel, (requests, head_width + lanes), F32, [VMEM] * 4, limit=16 * MIB,
        flops=2 * requests * feature_rows * (head_width + lanes),
        moved=2 * feature_rows * (head_width + lanes),
    )(columns, norm_gain.reshape(shape), query_weight, pair_weight)
    distance = 1
    while distance < requests:
        other = exchanged(sums, distance, requests)
        distance *= 2
        if distance < requests:
            sums = sums + other

    part = attend(requests, sums, other, cache[0], slot_request, slot_block, cache_lengths)
    distance = 1
    while distance < requests:
        other = exchanged(part, distance, requests)
        distance *= 2
        if distance < requests:
            part = call(merge_kernel, part.shape, F32, [VMEM] * 2, moved=16 * MIB)(part, other)

    columns_out = w_out.shape[2]
    projected = call(
        output_kernel, (sizes["kv"], requests * columns_out // LANES, LANES), F32, [VMEM] * 3,
        [pltpu.VMEM((rows, dim), F32)],
        limit=16 * MIB,
        flops=2 * requests * head_width * columns_out,
        moved=2 * head_width * columns_out,
    )(part, other, w_out[0])
    terms = lax.all_to_all(
        projected.reshape(sizes["kv"] * requests, columns_out // LANES, LANES),
        ("kv", "req"), 0, 0, tiled=True,
    )
    terms = terms.reshape(sizes["kv"], -1)
    return jnp.sum(terms, axis=0, keepdims=True).astype(BF16)


def solution(mesh):
    placed = (
        P(("parts", "req"), None),
        P(),
        P("req", "kv", None),
        P("req", "kv", None),
        P("kv", None, "req"),
        P("kv", ("parts", "req"), None, None),
        P(("parts", "req")),
        P(("parts", "req")),
        P("parts"),
    )
    return jax.shard_map(
        functools.partial(on_device, dict(mesh.shape)),
        mesh=mesh, in_specs=placed, out_specs=P(("parts", "req"), None), check_vma=False,
    )
```

```python
import functools

import jax
import jax.numpy as jnp
from jax import lax
from jax.experimental import pallas as pl
from jax.experimental.pallas import tpu as pltpu
from jax.sharding import PartitionSpec as P

LANES = 128
EMPTY = -1e30
F32 = jnp.float32
BF16 = jnp.bfloat16
VMEM = pl.BlockSpec(memory_space=pltpu.VMEM)
SMEM = pl.BlockSpec(memory_space=pltpu.SMEM)
MIB = 1024 * 1024


def spread_kernel(hidden_ref, out_ref):
    for row in range(out_ref.shape[0]):
        out_ref[row : row + 1, :] = hidden_ref[:, row * LANES : (row + 1) * LANES].astype(F32)


def scale_kernel(x_ref, out_ref):
    x = x_ref[...]
    mean = jnp.sum(jnp.sum(x * x, axis=0, keepdims=True), axis=1, keepdims=True) / x.size
    out_ref[...] = x * lax.rsqrt(mean + 1e-05)


def project_kernel(x_ref, gain_ref, query_ref, pair_ref, out_ref):
    chunks = x_ref.shape[1]
    me = lax.axis_index("req").astype(jnp.int32)
    gain = gain_ref[pl.ds(pl.multiple_of(me * chunks, chunks), chunks), :]
    x = x_ref[...] * gain[None]
    x = jnp.concatenate([x[:, chunk, :] for chunk in range(chunks)], axis=1).astype(BF16)
    width = query_ref.shape[1]
    step = 512
    for at in range(0, width, step):
        out_ref[:, at : at + step] = jnp.dot(
            x, query_ref[:, at : at + step], preferred_element_type=F32
        )
    out_ref[:, width:] = jnp.dot(x, pair_ref[...], preferred_element_type=F32)


def spread_sum_kernel(first_ref, second_ref, out_ref):
    total = first_ref[...] + second_ref[...]
    for copy in range(out_ref.shape[0]):
        out_ref[copy, :, :] = total


def attend_kernel(
    owner_ref, block_ref, length_ref, parts_ref, cache_ref, out_ref,
    wide, query, new_key, new_value, top, total, summed,
):
    near, requests, width = parts_ref.shape
    slots, tokens, lanes = cache_ref.shape
    dim = lanes // 2
    heads = (width - lanes) // dim

    def summed_parts(at):
        so_far = parts_ref[0, :, at]
        for index in range(1, near):
            so_far = so_far + parts_ref[index, :, at]
        return so_far

    scale = dim ** (-0.5)
    rows = requests * heads
    for head in range(heads):
        at = slice(head * dim, (head + 1) * dim)
        wide[pl.ds(head, requests, stride=heads), :] = summed_parts(at)
    query[...] = wide[...].astype(BF16)
    for new, start in ((new_key, heads * dim), (new_value, heads * dim + dim)):
        at = slice(start, start + dim)
        new[...] = summed_parts(at).astype(BF16).astype(F32)

    me = lax.axis_index("req").astype(jnp.int32)
    mine = pl.ds(pl.multiple_of(me * heads, heads), heads)
    own_key = new_key[pl.ds(me, 1), :]
    own_value = new_value[pl.ds(me, 1), :]
    own_score = (
        jnp.sum(query[mine, :].astype(F32) * own_key, axis=1, keepdims=True) * scale
    )
    top[...] = jnp.full(top.shape, EMPTY, F32)
    total[...] = jnp.zeros(total.shape, F32)
    summed[...] = jnp.zeros(summed.shape, F32)
    top[mine, :] = jnp.broadcast_to(own_score, (heads, dim))

    token = lax.broadcasted_iota(jnp.int32, (heads, tokens), 1)
    owners = [owner_ref[slot] for slot in range(slots)]
    sources = [jnp.maximum(owner, 0) for owner in owners]
    lives = [
        jnp.where(owners[slot] >= 0, length_ref[sources[slot]] - block_ref[slot] * tokens, 0)
        for slot in range(slots)
    ]
    places = [
        pl.ds(pl.multiple_of(jnp.where(owner >= 0, owner, requests) * heads, heads), heads)
        for owner in owners
    ]
    scores = [
        lax.dot_general(
            query[pl.ds(pl.multiple_of(sources[slot] * heads, heads), heads), :],
            cache_ref[slot, :, :dim],
            (((1,), (1,)), ((), ())),
            preferred_element_type=F32,
        )
        for slot in range(slots)
    ]
    masked = [jnp.where(token < lives[slot], scores[slot] * scale, EMPTY) for slot in range(slots)]
    maxima = [jnp.max(masked[slot], axis=1, keepdims=True) for slot in range(slots)]
    for slot in range(slots):
        top[places[slot], :] = jnp.maximum(top[places[slot], :], maxima[slot])
    weights = [jnp.exp(masked[slot] - maxima[slot]) for slot in range(slots)]
    outs = [
        jnp.dot(weights[slot].astype(BF16), cache_ref[slot, :, dim:], preferred_element_type=F32)
        for slot in range(slots)
    ]
    sums = [jnp.sum(weights[slot], axis=1, keepdims=True) for slot in range(slots)]
    factors = [jnp.exp(maxima[slot] - top[places[slot], :]) for slot in range(slots)]
    for slot in range(slots):
        place = places[slot]
        total[place, :] = total[place, :] + factors[slot] * sums[slot]
        summed[place, :] = summed[place, :] + factors[slot] * outs[slot]
    own_factor = jnp.exp(own_score - top[mine, :])
    total[mine, :] = total[mine, :] + own_factor
    summed[mine, :] = summed[mine, :] + own_factor * own_value

    out_ref[:dim, :] = summed[:rows, :].T
    out_ref[dim : dim + 1, :] = top[:rows, :].T[:1, :]
    out_ref[dim + 1 : dim + 2, :] = total[:rows, :].T[:1, :]
    out_ref[dim + 2 :, :] = jnp.zeros((out_ref.shape[0] - dim - 2, rows), F32)


def merged(parts):
    dim = LANES
    tops = [part[dim : dim + 1, :] for part in parts]
    top = tops[0]
    for other in tops[1:]:
        top = jnp.maximum(top, other)
    total = None
    summed = None
    for part, part_top in zip(parts, tops):
        factor = jnp.exp(part_top - top)
        part_total = part[dim + 1 : dim + 2, :] * factor
        part_summed = part[:dim, :] * factor
        total = part_total if total is None else total + part_total
        summed = part_summed if summed is None else summed + part_summed
    return top, total, summed


def merge_kernel(first_ref, second_ref, out_ref):
    dim = LANES
    top, total, summed = merged([first_ref, second_ref])
    for copy in range(out_ref.shape[0]):
        out_ref[copy, :dim, :] = summed
        out_ref[copy, dim : dim + 1, :] = top
        out_ref[copy, dim + 1 : dim + 2, :] = total
        out_ref[copy, dim + 2 :, :] = jnp.zeros((out_ref.shape[1] - dim - 2, out_ref.shape[2]), F32)


def output_kernel(parts_ref, weight_ref, out_ref, rows):
    _, total, summed = merged([parts_ref.at[index] for index in range(parts_ref.shape[0])])
    rows[...] = (summed / total).T
    heads = weight_ref.shape[0] // LANES
    requests = rows.shape[0] // heads
    x = jnp.concatenate(
        [rows[pl.ds(head, requests, stride=heads), :] for head in range(heads)], axis=1
    ).astype(BF16)
    width = weight_ref.shape[1]
    chunks = width // LANES
    step = min(512, width)
    for at in range(0, width, step):
        y = jnp.dot(x, weight_ref[:, at : at + step], preferred_element_type=F32)
        for chunk in range(step // LANES):
            part = y[:, chunk * LANES : (chunk + 1) * LANES]
            out_ref[pl.ds(at // LANES + chunk, requests, stride=chunks), :] = part


def round_sum_kernel(first_ref, second_ref, out_ref):
    out_ref[...] = (first_ref[...] + second_ref[...]).astype(BF16)


def call(kernel, shape, dtype, in_specs, scratch=(), limit=4 * MIB, flops=0, moved=0):
    return pl.pallas_call(
        kernel,
        out_shape=jax.ShapeDtypeStruct(shape, dtype),
        in_specs=in_specs,
        out_specs=VMEM,
        scratch_shapes=list(scratch),
        compiler_params=pltpu.CompilerParams(vmem_limit_bytes=limit),
        cost_estimate=pl.CostEstimate(flops=flops, bytes_accessed=moved, transcendentals=0),
    )


def exchanged(x, distance, size):
    return lax.ppermute(x, "req", [(place, place ^ distance) for place in range(size)])


def attend(requests, parts, cache, slot_request, slot_block, cache_lengths):
    slots, tokens, lanes = cache.shape
    dim = lanes // 2
    heads = (parts.shape[2] - lanes) // dim
    rows = requests * heads
    return call(
        attend_kernel, (dim + 8, rows), F32, [SMEM] * 3 + [VMEM] * 2,
        [
            pltpu.VMEM((rows, dim), F32),
            pltpu.VMEM((rows, dim), BF16),
            pltpu.VMEM((requests, dim), F32),
            pltpu.VMEM((requests, dim), F32),
            pltpu.VMEM((rows + heads, dim), F32),
            pltpu.VMEM((rows + heads, dim), F32),
            pltpu.VMEM((rows + heads, dim), F32),
        ],
        limit=16 * MIB,
        flops=2 * slots * tokens * heads * lanes,
        moved=2 * slots * tokens * lanes,
    )(slot_request, slot_block, cache_lengths, parts, cache)


def on_device(
    sizes, hidden, norm_gain, w_query, w_keyval, w_out, cache, slot_request, slot_block, cache_lengths
):
    requests = sizes["req"]
    features = hidden.shape[1]
    feature_rows = features // requests
    query_weight = w_query.reshape(feature_rows, -1)
    pair_weight = w_keyval.reshape(feature_rows, -1)
    head_width = query_weight.shape[1]
    lanes = pair_weight.shape[1]
    dim = lanes // 2
    rows = requests * head_width // dim

    shape = (features // LANES, LANES)
    spread = call(spread_kernel, shape, F32, [VMEM])(hidden)
    scaled = call(scale_kernel, shape, F32, [VMEM], flops=10**11)(spread)
    columns = lax.all_to_all(
        scaled.reshape(requests, feature_rows // LANES, LANES), "req", 0, 0, tiled=True
    )
    sums = call(
        project_kernel, (requests, head_width + lanes), F32, [VMEM] * 4, limit=16 * MIB,
        flops=2 * requests * feature_rows * (head_width + lanes),
        moved=2 * feature_rows * (head_width + lanes),
    )(columns, norm_gain.reshape(shape), query_weight, pair_weight)
    near = min(4, requests)
    groups = [list(range(at, at + near)) for at in range(0, requests, near)]

    def far_then_near(x, combine, combine_and_copy):
        distance = requests // 2
        while distance > near:
            x = combine(x, exchanged(x, distance, requests))
            distance //= 2
        x = combine_and_copy(x, exchanged(x, distance, requests))
        return lax.all_to_all(x, "req", 0, 0, tiled=True, axis_index_groups=groups)

    sums = far_then_near(
        sums, lambda x, y: x + y,
        lambda x, y: call(spread_sum_kernel, (near,) + x.shape, F32, [VMEM] * 2)(x, y),
    )
    part = attend(requests, sums, cache[0], slot_request, slot_block, cache_lengths)

    def merge(x, y, copies):
        return call(merge_kernel, (copies,) + x.shape, F32, [VMEM] * 2, moved=16 * MIB)(x, y)

    parts = far_then_near(part, lambda x, y: merge(x, y, 1)[0], lambda x, y: merge(x, y, near))

    columns_out = w_out.shape[2]
    projected = call(
        output_kernel, (requests * columns_out // LANES, LANES), F32, [VMEM] * 2,
        [pltpu.VMEM((rows, dim), F32)],
        limit=16 * MIB,
        flops=2 * requests * head_width * columns_out,
        moved=2 * head_width * columns_out,
    )(parts, w_out[0])
    other = lax.ppermute(projected, "kv", [(0, 1), (1, 0)])
    total = call(round_sum_kernel, projected.shape, BF16, [VMEM] * 2)(projected, other)
    result = lax.all_to_all(
        total.reshape(requests, columns_out // LANES, LANES), "req", 0, 0, tiled=True
    )
    return result.reshape(1, -1)


def solution(mesh):
    placed = (
        P(("parts", "req"), None),
        P(),
        P("req", "kv", None),
        P("req", "kv", None),
        P("kv", None, "req"),
        P("kv", ("parts", "req"), None, None),
        P(("parts", "req")),
        P(("parts", "req")),
        P("parts"),
    )
    return jax.shard_map(
        functools.partial(on_device, dict(mesh.shape)),
        mesh=mesh, in_specs=placed, out_specs=P(("parts", "req"), None), check_vma=False,
    )
```

```python
import functools

import jax
import jax.numpy as jnp
from jax import lax
from jax.experimental import pallas as pl
from jax.experimental.pallas import tpu as pltpu
from jax.sharding import PartitionSpec as P

LANES = 128
EMPTY = -1e30
F32 = jnp.float32
BF16 = jnp.bfloat16
VMEM = pl.BlockSpec(memory_space=pltpu.VMEM)
SMEM = pl.BlockSpec(memory_space=pltpu.SMEM)
MIB = 1024 * 1024


def spread_kernel(hidden_ref, out_ref):
    for row in range(out_ref.shape[0]):
        out_ref[row : row + 1, :] = hidden_ref[:, row * LANES : (row + 1) * LANES].astype(F32)


def scale_kernel(x_ref, out_ref):
    x = x_ref[...]
    mean = jnp.sum(jnp.sum(x * x, axis=0, keepdims=True), axis=1, keepdims=True) / x.size
    out_ref[...] = x * lax.rsqrt(mean + 1e-05)


def project_kernel(x_ref, gain_ref, query_ref, pair_ref, out_ref):
    chunks = x_ref.shape[1]
    me = lax.axis_index("req").astype(jnp.int32)
    gain = gain_ref[pl.ds(pl.multiple_of(me * chunks, chunks), chunks), :]
    x = x_ref[...] * gain[None]
    x = jnp.concatenate([x[:, chunk, :] for chunk in range(chunks)], axis=1).astype(BF16)
    width = query_ref.shape[1]
    step = 512
    for at in range(0, width, step):
        y = jnp.dot(x, query_ref[:, at : at + step], preferred_element_type=F32)
        for copy in range(out_ref.shape[0]):
            out_ref[copy, :, at : at + step] = y
    y = jnp.dot(x, pair_ref[...], preferred_element_type=F32)
    for copy in range(out_ref.shape[0]):
        out_ref[copy, :, width:] = y


def sum_kernel(parts_ref, out_ref):
    total = parts_ref[0]
    for index in range(1, parts_ref.shape[0]):
        total = total + parts_ref[index]
    out_ref[...] = total


def slots_kernel(owner_ref, block_ref, length_ref, place_ref, pick_ref, live_ref, tokens):
    slots = owner_ref.shape[0]
    requests = length_ref.shape[0]
    lane = lax.broadcasted_iota(jnp.int32, place_ref.shape, 1)
    places = jnp.zeros(place_ref.shape, jnp.int32)
    heads = pick_ref.shape[0] // slots
    shape = (heads, pick_ref.shape[1])
    offset = lax.broadcasted_iota(jnp.int32, shape, 1) - lax.broadcasted_iota(jnp.int32, shape, 0)
    for slot in range(slots):
        owner = owner_ref[slot]
        live = jnp.where(
            owner >= 0, length_ref[jnp.maximum(owner, 0)] - block_ref[slot] * tokens, 0
        )
        place = jnp.where(owner >= 0, owner, requests) * heads
        places = jnp.where(lane == slot, place, places)
        rows = slice(slot * heads, (slot + 1) * heads)
        pick_ref[rows, :] = jnp.where(offset == owner * heads, 1.0, 0.0).astype(BF16)
        live_ref[rows, :] = jnp.full((heads, LANES), live, jnp.int32)
    place_ref[...] = places


def keys_kernel(cache_ref, out_ref):
    dim = out_ref.shape[1]
    for slot in range(cache_ref.shape[0]):
        out_ref[slot, :, :] = cache_ref[slot, :, :dim].T


def attend_kernel(
    place_ref, pick_ref, live_ref, first_ref, second_ref, key_ref, cache_ref, out_ref,
    wide, query, new_key, new_value, top, total, summed,
):
    requests, width = first_ref.shape
    slots, tokens, lanes = cache_ref.shape
    dim = lanes // 2
    heads = (width - lanes) // dim

    def summed_parts(at):
        return first_ref[:, at] + second_ref[:, at]

    scale = dim ** (-0.5)
    rows = requests * heads
    for head in range(heads):
        at = slice(head * dim, (head + 1) * dim)
        wide[pl.ds(head, requests, stride=heads), :] = summed_parts(at)
    query[...] = wide[...].astype(BF16)
    for new, start in ((new_key, heads * dim), (new_value, heads * dim + dim)):
        at = slice(start, start + dim)
        new[...] = summed_parts(at).astype(BF16).astype(F32)

    me = lax.axis_index("req").astype(jnp.int32)
    mine = pl.ds(pl.multiple_of(me * heads, heads), heads)
    own_key = new_key[pl.ds(me, 1), :]
    own_value = new_value[pl.ds(me, 1), :]
    own_score = (
        jnp.sum(query[mine, :].astype(F32) * own_key, axis=1, keepdims=True) * scale
    )
    top[...] = jnp.full(top.shape, EMPTY, F32)
    total[...] = jnp.zeros(total.shape, F32)
    summed[...] = jnp.zeros(summed.shape, F32)
    top[mine, :] = jnp.broadcast_to(own_score, (heads, dim))

    slot_query = jnp.dot(pick_ref[...], query[...], preferred_element_type=F32).astype(BF16)
    scores = [
        jnp.dot(
            slot_query[slot * heads : (slot + 1) * heads, :],
            key_ref[slot, :, :],
            preferred_element_type=F32,
        )
        for slot in range(slots)
    ]
    token = lax.broadcasted_iota(jnp.int32, (heads, tokens), 1)
    lives = [
        jnp.concatenate([live_ref[slot * heads : (slot + 1) * heads, :]] * (tokens // LANES), axis=1)
        for slot in range(slots)
    ]
    masked = [jnp.where(token < lives[slot], scores[slot] * scale, EMPTY) for slot in range(slots)]
    maxima = [jnp.max(masked[slot], axis=1, keepdims=True) for slot in range(slots)]
    starts = place_ref[:1, :]
    places = [pl.ds(pl.multiple_of(starts[0, slot], heads), heads) for slot in range(slots)]
    for slot in range(slots):
        top[places[slot], :] = jnp.maximum(top[places[slot], :], maxima[slot])
    weights = [jnp.exp(masked[slot] - maxima[slot]) for slot in range(slots)]
    outs = [
        jnp.dot(weights[slot].astype(BF16), cache_ref[slot, :, dim:], preferred_element_type=F32)
        for slot in range(slots)
    ]
    sums = [jnp.sum(weights[slot], axis=1, keepdims=True) for slot in range(slots)]
    factors = [jnp.exp(maxima[slot] - top[places[slot], :]) for slot in range(slots)]
    for slot in range(slots):
        place = places[slot]
        total[place, :] = total[place, :] + factors[slot] * sums[slot]
        summed[place, :] = summed[place, :] + factors[slot] * outs[slot]
    own_factor = jnp.exp(own_score - top[mine, :])
    total[mine, :] = total[mine, :] + own_factor
    summed[mine, :] = summed[mine, :] + own_factor * own_value

    out_ref[:dim, :] = summed[:rows, :].T
    out_ref[dim : dim + 1, :] = top[:rows, :].T[:1, :]
    out_ref[dim + 1 : dim + 2, :] = total[:rows, :].T[:1, :]
    out_ref[dim + 2 :, :] = jnp.zeros((out_ref.shape[0] - dim - 2, rows), F32)


def merged(parts):
    dim = LANES
    tops = [part[dim : dim + 1, :] for part in parts]
    top = tops[0]
    for other in tops[1:]:
        top = jnp.maximum(top, other)
    total = None
    summed = None
    for part, part_top in zip(parts, tops):
        factor = jnp.exp(part_top - top)
        part_total = part[dim + 1 : dim + 2, :] * factor
        part_summed = part[:dim, :] * factor
        total = part_total if total is None else total + part_total
        summed = part_summed if summed is None else summed + part_summed
    return top, total, summed


def merge_kernel(first_ref, second_ref, out_ref):
    dim = LANES
    top, total, summed = merged([first_ref, second_ref])
    for copy in range(out_ref.shape[0]):
        out_ref[copy, :dim, :] = summed
        out_ref[copy, dim : dim + 1, :] = top
        out_ref[copy, dim + 1 : dim + 2, :] = total
        out_ref[copy, dim + 2 :, :] = jnp.zeros((out_ref.shape[1] - dim - 2, out_ref.shape[2]), F32)


def output_kernel(parts_ref, weight_ref, out_ref, rows):
    _, total, summed = merged([parts_ref.at[index] for index in range(parts_ref.shape[0])])
    rows[...] = (summed / total).T
    heads = weight_ref.shape[0] // LANES
    requests = rows.shape[0] // heads
    x = jnp.concatenate(
        [rows[pl.ds(head, requests, stride=heads), :] for head in range(heads)], axis=1
    ).astype(BF16)
    width = weight_ref.shape[1]
    chunks = width // LANES
    step = min(512, width)
    for at in range(0, width, step):
        y = jnp.dot(x, weight_ref[:, at : at + step], preferred_element_type=F32)
        for chunk in range(step // LANES):
            part = y[:, chunk * LANES : (chunk + 1) * LANES]
            out_ref[pl.ds(at // LANES + chunk, requests, stride=chunks), :] = part


def round_sum_kernel(first_ref, second_ref, out_ref):
    out_ref[...] = (first_ref[...] + second_ref[...]).astype(BF16)


def call(kernel, shape, dtype, in_specs, scratch=(), limit=4 * MIB, flops=0, moved=0):
    return pl.pallas_call(
        kernel,
        out_shape=jax.ShapeDtypeStruct(shape, dtype),
        in_specs=in_specs,
        out_specs=VMEM,
        scratch_shapes=list(scratch),
        compiler_params=pltpu.CompilerParams(vmem_limit_bytes=limit),
        cost_estimate=pl.CostEstimate(flops=flops, bytes_accessed=moved, transcendentals=0),
    )


def exchanged(x, distance, size):
    return lax.ppermute(x, "req", [(place, place ^ distance) for place in range(size)])


def slot_tables(heads, tokens, slot_request, slot_block, cache_lengths):
    slots = slot_request.shape[0]
    return pl.pallas_call(
        functools.partial(slots_kernel, tokens=tokens),
        out_shape=(
            jax.ShapeDtypeStruct((8, LANES), jnp.int32),
            jax.ShapeDtypeStruct((slots * heads, cache_lengths.shape[0] * heads), BF16),
            jax.ShapeDtypeStruct((slots * heads, LANES), jnp.int32),
        ),
        in_specs=[SMEM] * 3,
        out_specs=(VMEM,) * 3,
        compiler_params=pltpu.CompilerParams(vmem_limit_bytes=4 * MIB),
    )(slot_request, slot_block, cache_lengths)


def transposed_keys(cache):
    slots, tokens, lanes = cache.shape
    return call(
        keys_kernel, (slots, lanes // 2, tokens), BF16, [VMEM], limit=16 * MIB,
        moved=2 * slots * tokens * lanes,
    )(cache)


def attend(requests, first, second, keys, cache, place, pick, live):
    slots, tokens, lanes = cache.shape
    dim = lanes // 2
    heads = (first.shape[1] - lanes) // dim
    rows = requests * heads
    return call(
        attend_kernel, (dim + 8, rows), F32, [VMEM] * 7,
        [
            pltpu.VMEM((rows, dim), F32),
            pltpu.VMEM((rows, dim), BF16),
            pltpu.VMEM((requests, dim), F32),
            pltpu.VMEM((requests, dim), F32),
            pltpu.VMEM((rows + heads, dim), F32),
            pltpu.VMEM((rows + heads, dim), F32),
            pltpu.VMEM((rows + heads, dim), F32),
        ],
        limit=16 * MIB,
        flops=2 * slots * tokens * heads * lanes,
        moved=2 * slots * tokens * lanes,
    )(place, pick, live, first, second, keys, cache)


def swapped(x):
    return lax.ppermute(x, "kv", [(0, 1), (1, 0)])


def on_device(
    sizes, hidden, norm_gain, w_query, w_keyval, w_out, cache, slot_request, slot_block, cache_lengths
):
    requests = sizes["req"]
    features = hidden.shape[1]
    feature_rows = features // requests
    query_weight = w_query.reshape(feature_rows, -1)
    pair_weight = w_keyval.reshape(feature_rows, -1)
    head_width = query_weight.shape[1]
    lanes = pair_weight.shape[1]
    dim = lanes // 2
    rows = requests * head_width // dim

    shape = (features // LANES, LANES)
    spread = call(spread_kernel, shape, F32, [VMEM])(hidden)
    scaled = call(scale_kernel, shape, F32, [VMEM], flops=10**11)(spread)
    columns = lax.all_to_all(
        scaled.reshape(requests, feature_rows // LANES, LANES), "req", 0, 0, tiled=True
    )
    near = min(4, requests)
    groups = [list(range(at, at + near)) for at in range(0, requests, near)]
    sums = call(
        project_kernel, (near, requests, head_width + lanes), F32, [VMEM] * 4, limit=16 * MIB,
        flops=2 * requests * feature_rows * (head_width + lanes),
        moved=2 * feature_rows * (head_width + lanes),
    )(columns, norm_gain.reshape(shape), query_weight, pair_weight)
    near = min(4, requests)
    groups = [list(range(at, at + near)) for at in range(0, requests, near)]

    def crossed(x, distance):
        places = [(core, place) for core in range(2) for place in range(requests)]
        pairs = [
            (core * requests + place, (1 - core) * requests + (place ^ distance))
            for core, place in places
        ]
        return lax.ppermute(x, ("kv", "req"), pairs)

    def far_then_near(x, combine, cross):
        distance = requests // 2
        while distance >= near:
            if cross and distance == requests // 2:
                other = crossed(x, distance)
                x = swapped(x)
            else:
                other = exchanged(x, distance, requests)
            x = combine(x, other, near if distance == near else 1)
            distance //= 2
        return lax.all_to_all(x, "req", 0, 0, tiled=True, axis_index_groups=groups)

    def merge(x, y, copies):
        y = call(merge_kernel, (copies,) + x.shape, F32, [VMEM] * 2, moved=16 * MIB)(x, y)
        return y if copies > 1 else y[0]

    sums = lax.all_to_all(sums, "req", 0, 0, tiled=True, axis_index_groups=groups)
    sums = call(sum_kernel, sums.shape[1:], F32, [VMEM])(sums)
    distance = near
    while distance < requests:
        other = exchanged(sums, distance, requests)
        distance *= 2
        if distance < requests:
            sums = sums + other
    tables = slot_tables(
        head_width // dim, cache.shape[2], slot_request, slot_block, cache_lengths
    )
    keys = transposed_keys(cache[0])
    part = attend(requests, sums, other, keys, cache[0], *tables)
    parts = far_then_near(part, merge, True)

    columns_out = w_out.shape[2]
    projected = call(
        output_kernel, (requests * columns_out // LANES, LANES), F32, [VMEM] * 2,
        [pltpu.VMEM((rows, dim), F32)],
        limit=16 * MIB,
        flops=2 * requests * head_width * columns_out,
        moved=2 * head_width * columns_out,
    )(parts, swapped(w_out[0]))
    other = swapped(projected)
    total = call(round_sum_kernel, projected.shape, BF16, [VMEM] * 2)(projected, other)
    result = lax.all_to_all(
        total.reshape(requests, columns_out // LANES, LANES), "req", 0, 0, tiled=True
    )
    return result.reshape(1, -1)


def solution(mesh):
    placed = (
        P(("parts", "req"), None),
        P(),
        P("req", "kv", None),
        P("req", "kv", None),
        P("kv", None, "req"),
        P("kv", ("parts", "req"), None, None),
        P(("parts", "req")),
        P(("parts", "req")),
        P("parts"),
    )
    return jax.shard_map(
        functools.partial(on_device, dict(mesh.shape)),
        mesh=mesh, in_specs=placed, out_specs=P(("parts", "req"), None), check_vma=False,
    )
```

```python
import functools

import jax
import jax.numpy as jnp
from jax import lax
from jax.experimental import pallas as pl
from jax.experimental.pallas import tpu as pltpu
from jax.sharding import PartitionSpec as P

LANES = 128
EMPTY = -1e30
F32 = jnp.float32
BF16 = jnp.bfloat16
VMEM = pl.BlockSpec(memory_space=pltpu.VMEM)
SMEM = pl.BlockSpec(memory_space=pltpu.SMEM)
MIB = 1024 * 1024


def spread_kernel(hidden_ref, out_ref):
    for row in range(out_ref.shape[0]):
        out_ref[row : row + 1, :] = hidden_ref[:, row * LANES : (row + 1) * LANES].astype(F32)


def scale_kernel(x_ref, out_ref):
    x = x_ref[...]
    mean = jnp.sum(jnp.sum(x * x, axis=0, keepdims=True), axis=1, keepdims=True) / x.size
    out_ref[...] = x * lax.rsqrt(mean + 1e-05)


def project_kernel(x_ref, gain_ref, query_ref, pair_ref, out_ref):
    chunks = x_ref.shape[1]
    me = lax.axis_index("req").astype(jnp.int32)
    gain = gain_ref[pl.ds(pl.multiple_of(me * chunks, chunks), chunks), :]
    x = x_ref[...] * gain[None]
    x = jnp.concatenate([x[:, chunk, :] for chunk in range(chunks)], axis=1).astype(BF16)
    width = query_ref.shape[1]
    step = 512
    for at in range(0, width, step):
        y = jnp.dot(x, query_ref[:, at : at + step], preferred_element_type=F32)
        for copy in range(out_ref.shape[0]):
            out_ref[copy, :, at : at + step] = y
    y = jnp.dot(x, pair_ref[...], preferred_element_type=F32)
    near, requests = out_ref.shape[:2]
    unused = jnp.zeros((requests - 2 * (requests // near), LANES), F32)
    for copy in range(near):
        wanted = [y[at : at + 1, :] for at in range(copy, requests, near)]
        pairs = [row[:, :LANES] for row in wanted] + [row[:, LANES:] for row in wanted]
        out_ref[copy, :, width:] = jnp.concatenate(pairs + [unused], axis=0)


def sum_kernel(parts_ref, out_ref):
    total = parts_ref[0]
    for index in range(1, parts_ref.shape[0]):
        total = total + parts_ref[index]
    out_ref[...] = total


def slots_kernel(owner_ref, block_ref, length_ref, place_ref, pick_ref, live_ref, tokens):
    slots = owner_ref.shape[0]
    requests = length_ref.shape[0]
    lane = lax.broadcasted_iota(jnp.int32, place_ref.shape, 1)
    places = jnp.zeros(place_ref.shape, jnp.int32)
    heads = pick_ref.shape[0] // slots
    shape = (heads, pick_ref.shape[1])
    offset = lax.broadcasted_iota(jnp.int32, shape, 1) - lax.broadcasted_iota(jnp.int32, shape, 0)
    for slot in range(slots):
        owner = owner_ref[slot]
        live = jnp.where(
            owner >= 0, length_ref[jnp.maximum(owner, 0)] - block_ref[slot] * tokens, 0
        )
        place = jnp.where(owner >= 0, owner, requests) * heads
        places = jnp.where(lane == slot, place, places)
        rows = slice(slot * heads, (slot + 1) * heads)
        pick_ref[rows, :] = jnp.where(offset == owner * heads, 1.0, 0.0).astype(BF16)
        live_ref[rows, :] = jnp.full((heads, LANES), live, jnp.int32)
    place_ref[...] = places


def keys_kernel(cache_ref, out_ref):
    dim = out_ref.shape[1]
    for slot in range(cache_ref.shape[0]):
        out_ref[slot, :, :] = cache_ref[slot, :, :dim].T


def attend_kernel(
    place_ref, pick_ref, live_ref, first_ref, second_ref, key_ref, cache_ref, out_ref,
    wide, query, new_pair, top, total, summed,
):
    requests, width = first_ref.shape
    slots, tokens, lanes = cache_ref.shape
    dim = lanes // 2
    heads = width // dim - 1

    def summed_parts(at):
        return first_ref[:, at] + second_ref[:, at]

    scale = dim ** (-0.5)
    rows = requests * heads
    for head in range(heads):
        at = slice(head * dim, (head + 1) * dim)
        wide[pl.ds(head, requests, stride=heads), :] = summed_parts(at)
    query[...] = wide[...].astype(BF16)
    new_pair[...] = summed_parts(slice(heads * dim, width)).astype(BF16).astype(F32)

    me = lax.axis_index("req").astype(jnp.int32)
    mine = pl.ds(pl.multiple_of(me * heads, heads), heads)
    near = min(4, requests)
    own_key = new_pair[pl.ds(me // near, 1), :]
    own_value = new_pair[pl.ds(requests // near + me // near, 1), :]
    own_score = (
        jnp.sum(query[mine, :].astype(F32) * own_key, axis=1, keepdims=True) * scale
    )
    top[...] = jnp.full(top.shape, EMPTY, F32)
    total[...] = jnp.zeros(total.shape, F32)
    summed[...] = jnp.zeros(summed.shape, F32)
    top[mine, :] = jnp.broadcast_to(own_score, (heads, dim))

    slot_query = jnp.dot(pick_ref[...], query[...], preferred_element_type=F32).astype(BF16)
    scores = [
        jnp.dot(
            slot_query[slot * heads : (slot + 1) * heads, :],
            key_ref[slot, :, :],
            preferred_element_type=F32,
        )
        for slot in range(slots)
    ]
    token = lax.broadcasted_iota(jnp.int32, (heads, tokens), 1)
    lives = [
        jnp.concatenate([live_ref[slot * heads : (slot + 1) * heads, :]] * (tokens // LANES), axis=1)
        for slot in range(slots)
    ]
    masked = [jnp.where(token < lives[slot], scores[slot] * scale, EMPTY) for slot in range(slots)]
    maxima = [jnp.max(masked[slot], axis=1, keepdims=True) for slot in range(slots)]
    starts = place_ref[:1, :]
    places = [pl.ds(pl.multiple_of(starts[0, slot], heads), heads) for slot in range(slots)]
    for slot in range(slots):
        top[places[slot], :] = jnp.maximum(top[places[slot], :], maxima[slot])
    weights = [jnp.exp(masked[slot] - maxima[slot]) for slot in range(slots)]
    outs = [
        jnp.dot(weights[slot].astype(BF16), cache_ref[slot, :, dim:], preferred_element_type=F32)
        for slot in range(slots)
    ]
    sums = [jnp.sum(weights[slot], axis=1, keepdims=True) for slot in range(slots)]
    factors = [jnp.exp(maxima[slot] - top[places[slot], :]) for slot in range(slots)]
    for slot in range(slots):
        place = places[slot]
        total[place, :] = total[place, :] + factors[slot] * sums[slot]
        summed[place, :] = summed[place, :] + factors[slot] * outs[slot]
    own_factor = jnp.exp(own_score - top[mine, :])
    total[mine, :] = total[mine, :] + own_factor
    summed[mine, :] = summed[mine, :] + own_factor * own_value

    out_ref[:dim, :] = summed[:rows, :].T
    lane = lax.broadcasted_iota(jnp.int32, (rows, dim), 1)
    out_ref[dim : dim + 2, :] = jnp.where(lane == 0, top[:rows, :], total[:rows, :]).T[:2, :]
    out_ref[dim + 2 :, :] = jnp.zeros((out_ref.shape[0] - dim - 2, rows), F32)


def merged(parts):
    dim = LANES
    tops = [part[dim : dim + 1, :] for part in parts]
    top = tops[0]
    for other in tops[1:]:
        top = jnp.maximum(top, other)
    total = None
    summed = None
    for part, part_top in zip(parts, tops):
        factor = jnp.exp(part_top - top)
        part_total = part[dim + 1 : dim + 2, :] * factor
        part_summed = part[:dim, :] * factor
        total = part_total if total is None else total + part_total
        summed = part_summed if summed is None else summed + part_summed
    return top, total, summed


def merge_kernel(first_ref, second_ref, out_ref):
    dim = LANES
    top, total, summed = merged([first_ref, second_ref])
    for copy in range(out_ref.shape[0]):
        out_ref[copy, :dim, :] = summed
        out_ref[copy, dim : dim + 1, :] = top
        out_ref[copy, dim + 1 : dim + 2, :] = total
        out_ref[copy, dim + 2 :, :] = jnp.zeros((out_ref.shape[1] - dim - 2, out_ref.shape[2]), F32)


def output_kernel(parts_ref, weight_ref, out_ref, rows):
    _, total, summed = merged([parts_ref.at[index] for index in range(parts_ref.shape[0])])
    rows[...] = (summed / total).T
    heads = weight_ref.shape[0] // LANES
    requests = rows.shape[0] // heads
    x = jnp.concatenate(
        [rows[pl.ds(head, requests, stride=heads), :] for head in range(heads)], axis=1
    ).astype(BF16)
    width = weight_ref.shape[1]
    chunks = width // LANES
    step = min(512, width)
    for at in range(0, width, step):
        y = jnp.dot(x, weight_ref[:, at : at + step], preferred_element_type=F32)
        for chunk in range(step // LANES):
            part = y[:, chunk * LANES : (chunk + 1) * LANES]
            out_ref[pl.ds(at // LANES + chunk, requests, stride=chunks), :] = part


def round_sum_kernel(first_ref, second_ref, out_ref):
    out_ref[...] = (first_ref[...] + second_ref[...]).astype(BF16)


def call(kernel, shape, dtype, in_specs, scratch=(), limit=4 * MIB, flops=0, moved=0):
    return pl.pallas_call(
        kernel,
        out_shape=jax.ShapeDtypeStruct(shape, dtype),
        in_specs=in_specs,
        out_specs=VMEM,
        scratch_shapes=list(scratch),
        compiler_params=pltpu.CompilerParams(vmem_limit_bytes=limit),
        cost_estimate=pl.CostEstimate(flops=flops, bytes_accessed=moved, transcendentals=0),
    )


def exchanged(x, distance, size):
    return lax.ppermute(x, "req", [(place, place ^ distance) for place in range(size)])


def slot_tables(heads, tokens, slot_request, slot_block, cache_lengths):
    slots = slot_request.shape[0]
    return pl.pallas_call(
        functools.partial(slots_kernel, tokens=tokens),
        out_shape=(
            jax.ShapeDtypeStruct((8, LANES), jnp.int32),
            jax.ShapeDtypeStruct((slots * heads, cache_lengths.shape[0] * heads), BF16),
            jax.ShapeDtypeStruct((slots * heads, LANES), jnp.int32),
        ),
        in_specs=[SMEM] * 3,
        out_specs=(VMEM,) * 3,
        compiler_params=pltpu.CompilerParams(vmem_limit_bytes=4 * MIB),
    )(slot_request, slot_block, cache_lengths)


def transposed_keys(cache):
    slots, tokens, lanes = cache.shape
    return call(
        keys_kernel, (slots, lanes // 2, tokens), BF16, [VMEM], limit=16 * MIB,
        moved=2 * slots * tokens * lanes,
    )(cache)


def attend(requests, first, second, keys, cache, place, pick, live):
    slots, tokens, lanes = cache.shape
    dim = lanes // 2
    heads = first.shape[1] // dim - 1
    rows = requests * heads
    return call(
        attend_kernel, (dim + 8, rows), F32, [VMEM] * 7,
        [
            pltpu.VMEM((rows, dim), F32),
            pltpu.VMEM((rows, dim), BF16),
            pltpu.VMEM((requests, dim), F32),
            pltpu.VMEM((rows + heads, dim), F32),
            pltpu.VMEM((rows + heads, dim), F32),
            pltpu.VMEM((rows + heads, dim), F32),
        ],
        limit=16 * MIB,
        flops=2 * slots * tokens * heads * lanes,
        moved=2 * slots * tokens * lanes,
    )(place, pick, live, first, second, keys, cache)


def swapped(x):
    return lax.ppermute(x, "kv", [(0, 1), (1, 0)])


def on_device(
    sizes, hidden, norm_gain, w_query, w_keyval, w_out, cache, slot_request, slot_block, cache_lengths
):
    requests = sizes["req"]
    features = hidden.shape[1]
    feature_rows = features // requests
    query_weight = w_query.reshape(feature_rows, -1)
    pair_weight = w_keyval.reshape(feature_rows, -1)
    head_width = query_weight.shape[1]
    lanes = pair_weight.shape[1]
    dim = lanes // 2
    rows = requests * head_width // dim

    shape = (features // LANES, LANES)
    spread = call(spread_kernel, shape, F32, [VMEM])(hidden)
    scaled = call(scale_kernel, shape, F32, [VMEM], flops=10**11)(spread)
    columns = lax.all_to_all(
        scaled.reshape(requests, feature_rows // LANES, LANES), "req", 0, 0, tiled=True
    )
    near = min(4, requests)
    groups = [list(range(at, at + near)) for at in range(0, requests, near)]
    sums = call(
        project_kernel, (near, requests, head_width + dim), F32, [VMEM] * 4, limit=16 * MIB,
        flops=2 * requests * feature_rows * (head_width + lanes),
        moved=2 * feature_rows * (head_width + lanes),
    )(columns, norm_gain.reshape(shape), query_weight, pair_weight)
    near = min(4, requests)
    groups = [list(range(at, at + near)) for at in range(0, requests, near)]

    def crossed(x, distance):
        places = [(core, place) for core in range(2) for place in range(requests)]
        pairs = [
            (core * requests + place, (1 - core) * requests + (place ^ distance))
            for core, place in places
        ]
        return lax.ppermute(x, ("kv", "req"), pairs)

    def far_then_near(x, combine, cross):
        distance = requests // 2
        while distance >= near:
            if cross and distance == requests // 2:
                other = crossed(x, distance)
                x = swapped(x)
            else:
                other = exchanged(x, distance, requests)
            x = combine(x, other, near if distance == near else 1)
            distance //= 2
        return lax.all_to_all(x, "req", 0, 0, tiled=True, axis_index_groups=groups)

    def merge(x, y, copies):
        y = call(merge_kernel, (copies,) + x.shape, F32, [VMEM] * 2, moved=16 * MIB)(x, y)
        return y if copies > 1 else y[0]

    sums = lax.all_to_all(sums, "req", 0, 0, tiled=True, axis_index_groups=groups)
    sums = call(sum_kernel, sums.shape[1:], F32, [VMEM])(sums)
    distance = near
    while distance < requests:
        other = exchanged(sums, distance, requests)
        distance *= 2
        if distance < requests:
            sums = sums + other
    tables = slot_tables(
        head_width // dim, cache.shape[2], slot_request, slot_block, cache_lengths
    )
    keys = transposed_keys(cache[0])
    part = attend(requests, sums, other, keys, cache[0], *tables)
    parts = far_then_near(part, merge, True)

    columns_out = w_out.shape[2]
    projected = call(
        output_kernel, (requests * columns_out // LANES, LANES), F32, [VMEM] * 2,
        [pltpu.VMEM((rows, dim), F32)],
        limit=16 * MIB,
        flops=2 * requests * head_width * columns_out,
        moved=2 * head_width * columns_out,
    )(parts, swapped(w_out[0]))
    other = swapped(projected)
    total = call(round_sum_kernel, projected.shape, BF16, [VMEM] * 2)(projected, other)
    result = lax.all_to_all(
        total.reshape(requests, columns_out // LANES, LANES), "req", 0, 0, tiled=True
    )
    return result.reshape(1, -1)


def solution(mesh):
    placed = (
        P(("parts", "req"), None),
        P(),
        P("req", "kv", None),
        P("req", "kv", None),
        P("kv", None, "req"),
        P("kv", ("parts", "req"), None, None),
        P(("parts", "req")),
        P(("parts", "req")),
        P("parts"),
    )
    return jax.shard_map(
        functools.partial(on_device, dict(mesh.shape)),
        mesh=mesh, in_specs=placed, out_specs=P(("parts", "req"), None), check_vma=False,
    )
```

```python
import functools

import jax
import jax.numpy as jnp
from jax import lax
from jax.experimental import pallas as pl
from jax.experimental.pallas import tpu as pltpu
from jax.sharding import PartitionSpec as P

LANES = 128
EMPTY = -1e30
F32 = jnp.float32
BF16 = jnp.bfloat16
VMEM = pl.BlockSpec(memory_space=pltpu.VMEM)
SMEM = pl.BlockSpec(memory_space=pltpu.SMEM)
MIB = 1024 * 1024


def spread_kernel(hidden_ref, out_ref):
    for row in range(out_ref.shape[0]):
        out_ref[row : row + 1, :] = hidden_ref[:, row * LANES : (row + 1) * LANES].astype(F32)


def scale_kernel(x_ref, out_ref):
    x = x_ref[...]
    mean = jnp.sum(jnp.sum(x * x, axis=0, keepdims=True), axis=1, keepdims=True) / x.size
    out_ref[...] = x * lax.rsqrt(mean + 1e-05)


def project_kernel(x_ref, gain_ref, query_ref, pair_ref, out_ref):
    chunks = x_ref.shape[1]
    me = lax.axis_index("req").astype(jnp.int32)
    gain = gain_ref[pl.ds(pl.multiple_of(me * chunks, chunks), chunks), :]
    x = x_ref[...] * gain[None]
    x = jnp.concatenate([x[:, chunk, :] for chunk in range(chunks)], axis=1).astype(BF16)
    width = query_ref.shape[1]
    step = 1024
    for at in range(0, width, step):
        y = jnp.dot(x, query_ref[:, at : at + step], preferred_element_type=F32)
        for copy in range(out_ref.shape[0]):
            out_ref[copy, :, at : at + step] = y
    y = jnp.dot(x, pair_ref[...], preferred_element_type=F32)
    near, requests = out_ref.shape[:2]
    unused = jnp.zeros((requests - 2 * (requests // near), LANES), F32)
    for copy in range(near):
        wanted = [y[at : at + 1, :] for at in range(copy, requests, near)]
        pairs = [row[:, :LANES] for row in wanted] + [row[:, LANES:] for row in wanted]
        out_ref[copy, :, width:] = jnp.concatenate(pairs + [unused], axis=0)


def sum_kernel(parts_ref, out_ref):
    total = parts_ref[0]
    for index in range(1, parts_ref.shape[0]):
        total = total + parts_ref[index]
    out_ref[...] = total


def slots_kernel(owner_ref, block_ref, length_ref, place_ref, pick_ref, live_ref, tokens):
    slots = owner_ref.shape[0]
    requests = length_ref.shape[0]
    lane = lax.broadcasted_iota(jnp.int32, place_ref.shape, 1)
    places = jnp.zeros(place_ref.shape, jnp.int32)
    heads = pick_ref.shape[0] // slots
    shape = (heads, pick_ref.shape[1])
    offset = lax.broadcasted_iota(jnp.int32, shape, 1) - lax.broadcasted_iota(jnp.int32, shape, 0)
    for slot in range(slots):
        owner = owner_ref[slot]
        live = jnp.where(
            owner >= 0, length_ref[jnp.maximum(owner, 0)] - block_ref[slot] * tokens, 0
        )
        place = jnp.where(owner >= 0, owner, requests) * heads
        places = jnp.where(lane == slot, place, places)
        rows = slice(slot * heads, (slot + 1) * heads)
        pick_ref[rows, :] = jnp.where(offset == owner * heads, 1.0, 0.0).astype(BF16)
        live_ref[rows, :] = jnp.full((heads, LANES), live, jnp.int32)
    place_ref[...] = places


def keys_kernel(cache_ref, out_ref):
    dim = out_ref.shape[1]
    for slot in range(cache_ref.shape[0]):
        out_ref[slot, :, :] = cache_ref[slot, :, :dim].T


def attend_kernel(
    place_ref, pick_ref, live_ref, first_ref, second_ref, key_ref, cache_ref, out_ref,
    wide, query, new_pair, top, total, summed,
):
    requests, width = first_ref.shape
    slots, tokens, lanes = cache_ref.shape
    dim = lanes // 2
    heads = width // dim - 1

    def summed_parts(at):
        return first_ref[:, at] + second_ref[:, at]

    scale = dim ** (-0.5)
    rows = requests * heads
    for head in range(heads):
        at = slice(head * dim, (head + 1) * dim)
        wide[pl.ds(head, requests, stride=heads), :] = summed_parts(at)
    query[...] = wide[...].astype(BF16)
    new_pair[...] = summed_parts(slice(heads * dim, width)).astype(BF16).astype(F32)

    me = lax.axis_index("req").astype(jnp.int32)
    mine = pl.ds(pl.multiple_of(me * heads, heads), heads)
    near = min(4, requests)
    own_key = new_pair[pl.ds(me // near, 1), :]
    own_value = new_pair[pl.ds(requests // near + me // near, 1), :]
    own_score = (
        jnp.sum(query[mine, :].astype(F32) * own_key, axis=1, keepdims=True) * scale
    )
    top[...] = jnp.full(top.shape, EMPTY, F32)
    total[...] = jnp.zeros(total.shape, F32)
    summed[...] = jnp.zeros(summed.shape, F32)
    top[mine, :] = jnp.broadcast_to(own_score, (heads, dim))

    slot_query = jnp.dot(pick_ref[...], query[...], preferred_element_type=F32).astype(BF16)
    scores = [
        jnp.dot(
            slot_query[slot * heads : (slot + 1) * heads, :],
            key_ref[slot, :, :],
            preferred_element_type=F32,
        )
        for slot in range(slots)
    ]
    token = lax.broadcasted_iota(jnp.int32, (heads, tokens), 1)
    lives = [
        jnp.concatenate([live_ref[slot * heads : (slot + 1) * heads, :]] * (tokens // LANES), axis=1)
        for slot in range(slots)
    ]
    masked = [jnp.where(token < lives[slot], scores[slot] * scale, EMPTY) for slot in range(slots)]
    maxima = [jnp.max(masked[slot], axis=1, keepdims=True) for slot in range(slots)]
    starts = place_ref[:1, :]
    places = [pl.ds(pl.multiple_of(starts[0, slot], heads), heads) for slot in range(slots)]
    for slot in range(slots):
        top[places[slot], :] = jnp.maximum(top[places[slot], :], maxima[slot])
    weights = [jnp.exp(masked[slot] - maxima[slot]) for slot in range(slots)]
    outs = [
        jnp.dot(weights[slot].astype(BF16), cache_ref[slot, :, dim:], preferred_element_type=F32)
        for slot in range(slots)
    ]
    sums = [jnp.sum(weights[slot], axis=1, keepdims=True) for slot in range(slots)]
    factors = [jnp.exp(maxima[slot] - top[places[slot], :]) for slot in range(slots)]
    for slot in range(slots):
        place = places[slot]
        total[place, :] = total[place, :] + factors[slot] * sums[slot]
        summed[place, :] = summed[place, :] + factors[slot] * outs[slot]
    own_factor = jnp.exp(own_score - top[mine, :])
    total[mine, :] = total[mine, :] + own_factor
    summed[mine, :] = summed[mine, :] + own_factor * own_value

    out_ref[:dim, :] = summed[:rows, :].T
    lane = lax.broadcasted_iota(jnp.int32, (rows, dim), 1)
    out_ref[dim : dim + 2, :] = jnp.where(lane == 0, top[:rows, :], total[:rows, :]).T[:2, :]
    out_ref[dim + 2 :, :] = jnp.zeros((out_ref.shape[0] - dim - 2, rows), F32)


def merged(parts):
    dim = LANES
    tops = [part[dim : dim + 1, :] for part in parts]
    top = tops[0]
    for other in tops[1:]:
        top = jnp.maximum(top, other)
    total = None
    summed = None
    for part, part_top in zip(parts, tops):
        factor = jnp.exp(part_top - top)
        part_total = part[dim + 1 : dim + 2, :] * factor
        part_summed = part[:dim, :] * factor
        total = part_total if total is None else total + part_total
        summed = part_summed if summed is None else summed + part_summed
    return top, total, summed


def merge_kernel(first_ref, second_ref, out_ref):
    dim = LANES
    top, total, summed = merged([first_ref, second_ref])
    for copy in range(out_ref.shape[0]):
        out_ref[copy, :dim, :] = summed
        out_ref[copy, dim : dim + 1, :] = top
        out_ref[copy, dim + 1 : dim + 2, :] = total
        out_ref[copy, dim + 2 :, :] = jnp.zeros((out_ref.shape[1] - dim - 2, out_ref.shape[2]), F32)


def output_kernel(parts_ref, weight_ref, out_ref, rows):
    _, total, summed = merged([parts_ref.at[index] for index in range(parts_ref.shape[0])])
    rows[...] = (summed / total).T
    heads = weight_ref.shape[0] // LANES
    requests = rows.shape[0] // heads
    x = jnp.concatenate(
        [rows[pl.ds(head, requests, stride=heads), :] for head in range(heads)], axis=1
    ).astype(BF16)
    width = weight_ref.shape[1]
    chunks = width // LANES
    step = min(1024, width)
    for at in range(0, width, step):
        y = jnp.dot(x, weight_ref[:, at : at + step], preferred_element_type=F32)
        for chunk in range(step // LANES):
            part = y[:, chunk * LANES : (chunk + 1) * LANES]
            out_ref[pl.ds(at // LANES + chunk, requests, stride=chunks), :] = part


def round_sum_kernel(first_ref, second_ref, out_ref):
    out_ref[...] = (first_ref[...] + second_ref[...]).astype(BF16)


def call(kernel, shape, dtype, in_specs, scratch=(), limit=4 * MIB, flops=0, moved=0):
    return pl.pallas_call(
        kernel,
        out_shape=jax.ShapeDtypeStruct(shape, dtype),
        in_specs=in_specs,
        out_specs=VMEM,
        scratch_shapes=list(scratch),
        compiler_params=pltpu.CompilerParams(vmem_limit_bytes=limit),
        cost_estimate=pl.CostEstimate(flops=flops, bytes_accessed=moved, transcendentals=0),
    )


def exchanged(x, distance, size):
    return lax.ppermute(x, "req", [(place, place ^ distance) for place in range(size)])


def slot_tables(heads, tokens, slot_request, slot_block, cache_lengths):
    slots = slot_request.shape[0]
    return pl.pallas_call(
        functools.partial(slots_kernel, tokens=tokens),
        out_shape=(
            jax.ShapeDtypeStruct((8, LANES), jnp.int32),
            jax.ShapeDtypeStruct((slots * heads, cache_lengths.shape[0] * heads), BF16),
            jax.ShapeDtypeStruct((slots * heads, LANES), jnp.int32),
        ),
        in_specs=[SMEM] * 3,
        out_specs=(VMEM,) * 3,
        compiler_params=pltpu.CompilerParams(vmem_limit_bytes=4 * MIB),
    )(slot_request, slot_block, cache_lengths)


def transposed_keys(cache):
    slots, tokens, lanes = cache.shape
    return call(
        keys_kernel, (slots, lanes // 2, tokens), BF16, [VMEM], limit=16 * MIB,
        moved=2 * slots * tokens * lanes,
    )(cache)


def attend(requests, first, second, keys, cache, place, pick, live):
    slots, tokens, lanes = cache.shape
    dim = lanes // 2
    heads = first.shape[1] // dim - 1
    rows = requests * heads
    return call(
        attend_kernel, (dim + 8, rows), F32, [VMEM] * 7,
        [
            pltpu.VMEM((rows, dim), F32),
            pltpu.VMEM((rows, dim), BF16),
            pltpu.VMEM((requests, dim), F32),
            pltpu.VMEM((rows + heads, dim), F32),
            pltpu.VMEM((rows + heads, dim), F32),
            pltpu.VMEM((rows + heads, dim), F32),
        ],
        limit=16 * MIB,
        flops=2 * slots * tokens * heads * lanes,
        moved=2 * slots * tokens * lanes,
    )(place, pick, live, first, second, keys, cache)


def swapped(x):
    return lax.ppermute(x, "kv", [(0, 1), (1, 0)])


def on_device(
    sizes, hidden, norm_gain, w_query, w_keyval, w_out, cache, slot_request, slot_block, cache_lengths
):
    requests = sizes["req"]
    features = hidden.shape[1]
    feature_rows = features // requests
    query_weight = w_query.reshape(feature_rows, -1)
    pair_weight = w_keyval.reshape(feature_rows, -1)
    head_width = query_weight.shape[1]
    lanes = pair_weight.shape[1]
    dim = lanes // 2
    rows = requests * head_width // dim

    shape = (features // LANES, LANES)
    spread = call(spread_kernel, shape, F32, [VMEM])(hidden)
    scaled = call(scale_kernel, shape, F32, [VMEM], flops=10**11)(spread)
    columns = lax.all_to_all(
        scaled.reshape(requests, feature_rows // LANES, LANES), "req", 0, 0, tiled=True
    )
    near = min(4, requests)
    groups = [list(range(at, at + near)) for at in range(0, requests, near)]
    sums = call(
        project_kernel, (near, requests, head_width + dim), F32, [VMEM] * 4, limit=16 * MIB,
        flops=2 * requests * feature_rows * (head_width + lanes),
        moved=2 * feature_rows * (head_width + lanes),
    )(columns, norm_gain.reshape(shape), query_weight, pair_weight)
    near = min(4, requests)
    groups = [list(range(at, at + near)) for at in range(0, requests, near)]

    def crossed(x, distance):
        places = [(core, place) for core in range(2) for place in range(requests)]
        pairs = [
            (core * requests + place, (1 - core) * requests + (place ^ distance))
            for core, place in places
        ]
        return lax.ppermute(x, ("kv", "req"), pairs)

    def far_then_near(x, combine, cross):
        distance = requests // 2
        while distance >= near:
            if cross and distance == requests // 2:
                other = crossed(x, distance)
                x = swapped(x)
            else:
                other = exchanged(x, distance, requests)
            x = combine(x, other, near if distance == near else 1)
            distance //= 2
        return lax.all_to_all(x, "req", 0, 0, tiled=True, axis_index_groups=groups)

    def merge(x, y, copies):
        y = call(merge_kernel, (copies,) + x.shape, F32, [VMEM] * 2, moved=16 * MIB)(x, y)
        return y if copies > 1 else y[0]

    sums = lax.all_to_all(sums, "req", 0, 0, tiled=True, axis_index_groups=groups)
    sums = call(sum_kernel, sums.shape[1:], F32, [VMEM])(sums)
    distance = near
    while distance < requests:
        other = exchanged(sums, distance, requests)
        distance *= 2
        if distance < requests:
            sums = sums + other
    tables = slot_tables(
        head_width // dim, cache.shape[2], slot_request, slot_block, cache_lengths
    )
    keys = transposed_keys(cache[0])
    part = attend(requests, sums, other, keys, cache[0], *tables)
    parts = far_then_near(part, merge, True)

    columns_out = w_out.shape[2]
    projected = call(
        output_kernel, (requests * columns_out // LANES, LANES), F32, [VMEM] * 2,
        [pltpu.VMEM((rows, dim), F32)],
        limit=16 * MIB,
        flops=2 * requests * head_width * columns_out,
        moved=2 * head_width * columns_out,
    )(parts, swapped(w_out[0]))
    other = swapped(projected)
    total = call(round_sum_kernel, projected.shape, BF16, [VMEM] * 2)(projected, other)
    result = lax.all_to_all(
        total.reshape(requests, columns_out // LANES, LANES), "req", 0, 0, tiled=True
    )
    return result.reshape(1, -1)


def solution(mesh):
    placed = (
        P(("parts", "req"), None),
        P(),
        P("req", "kv", None),
        P("req", "kv", None),
        P("kv", None, "req"),
        P("kv", ("parts", "req"), None, None),
        P(("parts", "req")),
        P(("parts", "req")),
        P("parts"),
    )
    return jax.shard_map(
        functools.partial(on_device, dict(mesh.shape)),
        mesh=mesh, in_specs=placed, out_specs=P(("parts", "req"), None), check_vma=False,
    )
```

```python
import functools

import jax
import jax.numpy as jnp
from jax import lax
from jax.experimental import pallas as pl
from jax.experimental.pallas import tpu as pltpu
from jax.sharding import PartitionSpec as P

LANES = 128
EMPTY = -1e30
F32 = jnp.float32
BF16 = jnp.bfloat16
VMEM = pl.BlockSpec(memory_space=pltpu.VMEM)
SMEM = pl.BlockSpec(memory_space=pltpu.SMEM)
MIB = 1024 * 1024


def spread_kernel(hidden_ref, out_ref):
    for row in range(out_ref.shape[0]):
        out_ref[row : row + 1, :] = hidden_ref[:, row * LANES : (row + 1) * LANES].astype(F32)


def scale_kernel(x_ref, out_ref):
    x = x_ref[...]
    mean = jnp.sum(jnp.sum(x * x, axis=0, keepdims=True), axis=1, keepdims=True) / x.size
    out_ref[...] = x * lax.rsqrt(mean + 1e-05)


def project_kernel(x_ref, gain_ref, query_ref, pair_ref, out_ref):
    chunks = x_ref.shape[1]
    me = lax.axis_index("req").astype(jnp.int32)
    gain = gain_ref[pl.ds(pl.multiple_of(me * chunks, chunks), chunks), :]
    x = x_ref[...] * gain[None]
    x = jnp.concatenate([x[:, chunk, :] for chunk in range(chunks)], axis=1).astype(BF16)
    width = query_ref.shape[1]
    step = width
    for at in range(0, width, step):
        y = jnp.dot(x, query_ref[:, at : at + step], preferred_element_type=F32)
        for copy in range(out_ref.shape[0]):
            out_ref[copy, :, at : at + step] = y
    y = jnp.dot(x, pair_ref[...], preferred_element_type=F32)
    near, requests = out_ref.shape[:2]
    unused = jnp.zeros((requests - 2 * (requests // near), LANES), F32)
    for copy in range(near):
        wanted = [y[at : at + 1, :] for at in range(copy, requests, near)]
        pairs = [row[:, :LANES] for row in wanted] + [row[:, LANES:] for row in wanted]
        out_ref[copy, :, width:] = jnp.concatenate(pairs + [unused], axis=0)


def sum_kernel(parts_ref, out_ref):
    total = parts_ref[0]
    for index in range(1, parts_ref.shape[0]):
        total = total + parts_ref[index]
    out_ref[...] = total


def slots_kernel(owner_ref, block_ref, length_ref, place_ref, pick_ref, live_ref, tokens):
    slots = owner_ref.shape[0]
    requests = length_ref.shape[0]
    lane = lax.broadcasted_iota(jnp.int32, place_ref.shape, 1)
    places = jnp.zeros(place_ref.shape, jnp.int32)
    heads = pick_ref.shape[0] // slots
    shape = (heads, pick_ref.shape[1])
    offset = lax.broadcasted_iota(jnp.int32, shape, 1) - lax.broadcasted_iota(jnp.int32, shape, 0)
    for slot in range(slots):
        owner = owner_ref[slot]
        live = jnp.where(
            owner >= 0, length_ref[jnp.maximum(owner, 0)] - block_ref[slot] * tokens, 0
        )
        place = jnp.where(owner >= 0, owner, requests) * heads
        places = jnp.where(lane == slot, place, places)
        rows = slice(slot * heads, (slot + 1) * heads)
        pick_ref[rows, :] = jnp.where(offset == owner * heads, 1.0, 0.0).astype(BF16)
        live_ref[rows, :] = jnp.full((heads, LANES), live, jnp.int32)
    place_ref[...] = places


def keys_kernel(cache_ref, out_ref):
    dim = out_ref.shape[1]
    for slot in range(cache_ref.shape[0]):
        out_ref[slot, :, :] = cache_ref[slot, :, :dim].T


def attend_kernel(
    place_ref, pick_ref, live_ref, first_ref, second_ref, key_ref, cache_ref, out_ref,
    wide, query, new_pair, top, total, summed,
):
    requests, width = first_ref.shape
    slots, tokens, lanes = cache_ref.shape
    dim = lanes // 2
    heads = width // dim - 1

    def summed_parts(at):
        return first_ref[:, at] + second_ref[:, at]

    scale = dim ** (-0.5)
    rows = requests * heads
    for head in range(heads):
        at = slice(head * dim, (head + 1) * dim)
        wide[pl.ds(head, requests, stride=heads), :] = summed_parts(at)
    query[...] = wide[...].astype(BF16)
    new_pair[...] = summed_parts(slice(heads * dim, width)).astype(BF16).astype(F32)

    me = lax.axis_index("req").astype(jnp.int32)
    mine = pl.ds(pl.multiple_of(me * heads, heads), heads)
    near = min(4, requests)
    own_key = new_pair[pl.ds(me // near, 1), :]
    own_value = new_pair[pl.ds(requests // near + me // near, 1), :]
    own_score = (
        jnp.sum(query[mine, :].astype(F32) * own_key, axis=1, keepdims=True) * scale
    )
    top[...] = jnp.full(top.shape, EMPTY, F32)
    total[...] = jnp.zeros(total.shape, F32)
    summed[...] = jnp.zeros(summed.shape, F32)
    top[mine, :] = jnp.broadcast_to(own_score, (heads, dim))

    slot_query = jnp.dot(pick_ref[...], query[...], preferred_element_type=F32).astype(BF16)
    scores = [
        jnp.dot(
            slot_query[slot * heads : (slot + 1) * heads, :],
            key_ref[slot, :, :],
            preferred_element_type=F32,
        )
        for slot in range(slots)
    ]
    token = lax.broadcasted_iota(jnp.int32, (heads, tokens), 1)
    lives = [
        jnp.concatenate([live_ref[slot * heads : (slot + 1) * heads, :]] * (tokens // LANES), axis=1)
        for slot in range(slots)
    ]
    masked = [jnp.where(token < lives[slot], scores[slot] * scale, EMPTY) for slot in range(slots)]
    maxima = [jnp.max(masked[slot], axis=1, keepdims=True) for slot in range(slots)]
    starts = place_ref[:1, :]
    places = [pl.ds(pl.multiple_of(starts[0, slot], heads), heads) for slot in range(slots)]
    for slot in range(slots):
        top[places[slot], :] = jnp.maximum(top[places[slot], :], maxima[slot])
    weights = [jnp.exp(masked[slot] - maxima[slot]) for slot in range(slots)]
    outs = [
        jnp.dot(weights[slot].astype(BF16), cache_ref[slot, :, dim:], preferred_element_type=F32)
        for slot in range(slots)
    ]
    sums = [jnp.sum(weights[slot], axis=1, keepdims=True) for slot in range(slots)]
    factors = [jnp.exp(maxima[slot] - top[places[slot], :]) for slot in range(slots)]
    for slot in range(slots):
        place = places[slot]
        total[place, :] = total[place, :] + factors[slot] * sums[slot]
        summed[place, :] = summed[place, :] + factors[slot] * outs[slot]
    own_factor = jnp.exp(own_score - top[mine, :])
    total[mine, :] = total[mine, :] + own_factor
    summed[mine, :] = summed[mine, :] + own_factor * own_value

    out_ref[:dim, :] = summed[:rows, :].T
    lane = lax.broadcasted_iota(jnp.int32, (rows, dim), 1)
    out_ref[dim : dim + 2, :] = jnp.where(lane == 0, top[:rows, :], total[:rows, :]).T[:2, :]
    out_ref[dim + 2 :, :] = jnp.zeros((out_ref.shape[0] - dim - 2, rows), F32)


def merged(parts):
    dim = LANES
    tops = [part[dim : dim + 1, :] for part in parts]
    top = tops[0]
    for other in tops[1:]:
        top = jnp.maximum(top, other)
    total = None
    summed = None
    for part, part_top in zip(parts, tops):
        factor = jnp.exp(part_top - top)
        part_total = part[dim + 1 : dim + 2, :] * factor
        part_summed = part[:dim, :] * factor
        total = part_total if total is None else total + part_total
        summed = part_summed if summed is None else summed + part_summed
    return top, total, summed


def merge_kernel(first_ref, second_ref, out_ref):
    dim = LANES
    top, total, summed = merged([first_ref, second_ref])
    for copy in range(out_ref.shape[0]):
        out_ref[copy, :dim, :] = summed
        out_ref[copy, dim : dim + 1, :] = top
        out_ref[copy, dim + 1 : dim + 2, :] = total
        out_ref[copy, dim + 2 :, :] = jnp.zeros((out_ref.shape[1] - dim - 2, out_ref.shape[2]), F32)


def output_kernel(parts_ref, weight_ref, out_ref, rows):
    _, total, summed = merged([parts_ref.at[index] for index in range(parts_ref.shape[0])])
    rows[...] = (summed / total).T
    heads = weight_ref.shape[0] // LANES
    requests = rows.shape[0] // heads
    x = jnp.concatenate(
        [rows[pl.ds(head, requests, stride=heads), :] for head in range(heads)], axis=1
    ).astype(BF16)
    width = weight_ref.shape[1]
    chunks = width // LANES
    step = width
    for at in range(0, width, step):
        y = jnp.dot(x, weight_ref[:, at : at + step], preferred_element_type=F32)
        for chunk in range(step // LANES):
            part = y[:, chunk * LANES : (chunk + 1) * LANES]
            out_ref[pl.ds(at // LANES + chunk, requests, stride=chunks), :] = part


def round_sum_kernel(first_ref, second_ref, out_ref):
    out_ref[...] = (first_ref[...] + second_ref[...]).astype(BF16)


def call(kernel, shape, dtype, in_specs, scratch=(), limit=4 * MIB, flops=0, moved=0):
    return pl.pallas_call(
        kernel,
        out_shape=jax.ShapeDtypeStruct(shape, dtype),
        in_specs=in_specs,
        out_specs=VMEM,
        scratch_shapes=list(scratch),
        compiler_params=pltpu.CompilerParams(vmem_limit_bytes=limit),
        cost_estimate=pl.CostEstimate(flops=flops, bytes_accessed=moved, transcendentals=0),
    )


def exchanged(x, distance, size):
    return lax.ppermute(x, "req", [(place, place ^ distance) for place in range(size)])


def slot_tables(heads, tokens, slot_request, slot_block, cache_lengths):
    slots = slot_request.shape[0]
    return pl.pallas_call(
        functools.partial(slots_kernel, tokens=tokens),
        out_shape=(
            jax.ShapeDtypeStruct((8, LANES), jnp.int32),
            jax.ShapeDtypeStruct((slots * heads, cache_lengths.shape[0] * heads), BF16),
            jax.ShapeDtypeStruct((slots * heads, LANES), jnp.int32),
        ),
        in_specs=[SMEM] * 3,
        out_specs=(VMEM,) * 3,
        compiler_params=pltpu.CompilerParams(vmem_limit_bytes=4 * MIB),
    )(slot_request, slot_block, cache_lengths)


def transposed_keys(cache):
    slots, tokens, lanes = cache.shape
    return call(
        keys_kernel, (slots, lanes // 2, tokens), BF16, [VMEM], limit=16 * MIB,
        moved=2 * slots * tokens * lanes,
    )(cache)


def attend(requests, first, second, keys, cache, place, pick, live):
    slots, tokens, lanes = cache.shape
    dim = lanes // 2
    heads = first.shape[1] // dim - 1
    rows = requests * heads
    return call(
        attend_kernel, (dim + 8, rows), F32, [VMEM] * 7,
        [
            pltpu.VMEM((rows, dim), F32),
            pltpu.VMEM((rows, dim), BF16),
            pltpu.VMEM((requests, dim), F32),
            pltpu.VMEM((rows + heads, dim), F32),
            pltpu.VMEM((rows + heads, dim), F32),
            pltpu.VMEM((rows + heads, dim), F32),
        ],
        limit=16 * MIB,
        flops=2 * slots * tokens * heads * lanes,
        moved=2 * slots * tokens * lanes,
    )(place, pick, live, first, second, keys, cache)


def swapped(x):
    return lax.ppermute(x, "kv", [(0, 1), (1, 0)])


def on_device(
    sizes, hidden, norm_gain, w_query, w_keyval, w_out, cache, slot_request, slot_block, cache_lengths
):
    requests = sizes["req"]
    features = hidden.shape[1]
    feature_rows = features // requests
    query_weight = w_query.reshape(feature_rows, -1)
    pair_weight = w_keyval.reshape(feature_rows, -1)
    head_width = query_weight.shape[1]
    lanes = pair_weight.shape[1]
    dim = lanes // 2
    rows = requests * head_width // dim

    shape = (features // LANES, LANES)
    spread = call(spread_kernel, shape, F32, [VMEM])(hidden)
    scaled = call(scale_kernel, shape, F32, [VMEM], flops=10**11)(spread)
    columns = lax.all_to_all(
        scaled.reshape(requests, feature_rows // LANES, LANES), "req", 0, 0, tiled=True
    )
    near = min(4, requests)
    groups = [list(range(at, at + near)) for at in range(0, requests, near)]
    sums = call(
        project_kernel, (near, requests, head_width + dim), F32, [VMEM] * 4, limit=16 * MIB,
        flops=2 * requests * feature_rows * (head_width + lanes),
        moved=2 * feature_rows * (head_width + lanes),
    )(columns, norm_gain.reshape(shape), query_weight, pair_weight)
    near = min(4, requests)
    groups = [list(range(at, at + near)) for at in range(0, requests, near)]

    def crossed(x, distance):
        places = [(core, place) for core in range(2) for place in range(requests)]
        pairs = [
            (core * requests + place, (1 - core) * requests + (place ^ distance))
            for core, place in places
        ]
        return lax.ppermute(x, ("kv", "req"), pairs)

    def far_then_near(x, combine, cross):
        distance = requests // 2
        while distance >= near:
            if cross and distance == requests // 2:
                other = crossed(x, distance)
                x = swapped(x)
            else:
                other = exchanged(x, distance, requests)
            x = combine(x, other, near if distance == near else 1)
            distance //= 2
        return lax.all_to_all(x, "req", 0, 0, tiled=True, axis_index_groups=groups)

    def merge(x, y, copies):
        y = call(merge_kernel, (copies,) + x.shape, F32, [VMEM] * 2, moved=16 * MIB)(x, y)
        return y if copies > 1 else y[0]

    sums = lax.all_to_all(sums, "req", 0, 0, tiled=True, axis_index_groups=groups)
    sums = call(sum_kernel, sums.shape[1:], F32, [VMEM])(sums)
    distance = near
    while distance < requests:
        other = exchanged(sums, distance, requests)
        distance *= 2
        if distance < requests:
            sums = sums + other
    tables = slot_tables(
        head_width // dim, cache.shape[2], slot_request, slot_block, cache_lengths
    )
    keys = transposed_keys(cache[0])
    part = attend(requests, sums, other, keys, cache[0], *tables)
    parts = far_then_near(part, merge, True)

    columns_out = w_out.shape[2]
    projected = call(
        output_kernel, (requests * columns_out // LANES, LANES), F32, [VMEM] * 2,
        [pltpu.VMEM((rows, dim), F32)],
        limit=16 * MIB,
        flops=2 * requests * head_width * columns_out,
        moved=2 * head_width * columns_out,
    )(parts, swapped(w_out[0]))
    other = swapped(projected)
    total = call(round_sum_kernel, projected.shape, BF16, [VMEM] * 2)(projected, other)
    result = lax.all_to_all(
        total.reshape(requests, columns_out // LANES, LANES), "req", 0, 0, tiled=True
    )
    return result.reshape(1, -1)


def solution(mesh):
    placed = (
        P(("parts", "req"), None),
        P(),
        P("req", "kv", None),
        P("req", "kv", None),
        P("kv", None, "req"),
        P("kv", ("parts", "req"), None, None),
        P(("parts", "req")),
        P(("parts", "req")),
        P("parts"),
    )
    return jax.shard_map(
        functools.partial(on_device, dict(mesh.shape)),
        mesh=mesh, in_specs=placed, out_specs=P(("parts", "req"), None), check_vma=False,
    )
```
